32 devices in a mesh: join: 16 (over z, y, x), view: 2 (over core).
Axes of the slice: x: 2, y: 2, z: 4, core: 2. Of those that a mesh axis runs over, the one named last changes fastest.
Arguments:
- estimate: float32 [64, 256, 256], P('join', 'view'), may hold values from 0.5 to 2
- views: bfloat16 [64, 6, 256, 256], P('join', None, 'view'), may hold values from 0.25 to 4
- owners: int32 [64, 6], P('join'), may hold values from 0 to 15, all different within a row; in each aligned block of 4 rows (0 to 3, 4 to 7, ...) at most 3 rows name the same one
- local_blocks: int32 [64, 6], P('join'), may hold values from 0 to 3, as said below
- psf: float32 [6, 33], replicated, may hold values from 0.05 to 1
Outputs:
- deconvolved: float32 [64, 256, 256], P('join', 'view')
The draws below stay inside these ranges and needn't reach their ends.
Inputs may be any that keep to these rules, and one draw needn't show every extreme that they name: `owners`: each row names 6 different join indices; in the 4 rows of one join index no join index is named more than 3 times, and in every draw some join index is named exactly 3 times by some device's rows. `local_blocks`: in every draw one local block index, drawn from the seed and neither 0 nor 4 - 1, is named by no entry, so the estimate blocks with that index are imaged by no view; the other values all appear.
All inputs are finite; a program needn't handle non-finite values.
Results may differ from the reference program's by a relative error of at most 0.00065.
Values may be sent and summed in bfloat16 or wider, within the bound.
No kernel may reach another device: no remote copies, remote signals or barrier semaphores. Data moves between devices by JAX's collectives and lax.ppermute only.
A program may use at most 64 MiB of HBM per device.

```python
import math
import jax
import jax.numpy as jnp
import numpy as np
from jax import lax

VIEWS = 6
H = 16
R = 256
BXY_DEV = 4
CAP = 3
ITERS = 2
TAPS = 33
NBXY = 64
NZ = 256
N_JOIN = 16


def draw_local_blocks(key, part):
    key = jax.random.fold_in(key, 7)
    skip_key, rest_key = jax.random.split(key)
    skipped = jax.random.randint(skip_key, (), 1, BXY_DEV - 1)
    rest = jax.random.randint(rest_key, (NBXY, VIEWS), 0, BXY_DEV - 1)
    local = jnp.where(rest >= skipped, rest + 1, rest)
    local = local.at[0, 0].set(0)
    local = local.at[0, 1].set(BXY_DEV - 1)
    return local.astype(jnp.int32)


def shard_levels(stream_key, extent, shards, least, largest):
    gain, own = 1.0, jax.random.fold_in(stream_key, 6)
    for axis_at, blocks in shards:
        draws = jnp.exp(jax.random.uniform(jax.random.fold_in(own, axis_at), (blocks,), jnp.float32, least / len(shards), largest / len(shards)))
        gain = gain * jnp.repeat(draws, extent[axis_at] // blocks).reshape([-1 if axis == axis_at else 1 for axis in range(len(extent))])
    return gain


def routed_block(key, own, number, rows, amount, top, reach, lean):
    order = jax.random.permutation(key, amount)
    heavy_load, ordinary = portions_of(amount, rows * top, reach, lean, True), portions_of(amount, rows * top, reach, lean, False)
    places = jnp.arange(amount)

    def named(sizes, offset_by):
        used = int((sizes > 0).sum())
        fixed = max(1, used // 4)
        passed = fixed + (places - fixed + offset_by * (used - fixed)) % max(1, amount - fixed)
        return jnp.zeros((amount,), jnp.int32).at[order[jnp.where(places < fixed, places, passed)]].set(jnp.asarray(sizes, jnp.int32))

    sizes = jnp.where(number % 4 == 0, named(heavy_load, number // 4), named(ordinary, number - number // 4 - 1))
    mixed = jax.random.permutation(jax.random.fold_in(own, 3), amount)
    donor, receiver = mixed[0:amount // 2 * 2:2], mixed[1:amount // 2 * 2:2]
    slack = jnp.minimum(sizes[donor] - 1, reach - sizes[receiver]) // 2
    slack = jnp.where((donor == order[0]) | (receiver == order[0]) | (sizes[receiver] == 0), 0, jnp.maximum(slack, 0))
    passed = jax.random.randint(jax.random.fold_in(own, 4), (amount // 2,), 0, 1 << 20) % (slack + 1)
    sizes = sizes.at[donor].add(-passed).at[receiver].add(passed)
    items = jnp.searchsorted(jnp.cumsum(sizes), jnp.arange(rows * top), side="right").astype(jnp.int32)
    grid = items.reshape(top, rows).T
    grid = grid[jax.random.permutation(jax.random.fold_in(own, 1), rows)]
    offset_by = jax.random.randint(jax.random.fold_in(own, 2), (rows, 1), 0, top)
    return jnp.take_along_axis(grid, (jnp.arange(top)[None, :] + offset_by) % top, axis=1)


def portions_of(number_of, total, limit, skew, full):
    weights = [(1 << 20) // math.isqrt(standing ** skew) + 1 for standing in range(1, number_of + 1)]
    largest = limit if full else min(limit, max(-(-total // number_of), total * weights[0] // sum(weights)))
    least = 1 if total - largest >= number_of - 1 else 0
    given, spare = [largest] + [least] * (number_of - 1), total - largest - least * (number_of - 1)
    while spare > 0:
        movable = [i for i in range(1, number_of) if given[i] < largest] or [i for i in range(1, number_of) if given[i] < limit]
        whole, left = sum([weights[i] for i in movable]), spare
        for i in movable:
            addition = min(limit - given[i], max(1, left * weights[i] // whole), spare)
            given[i] = given[i] + addition
            spare = spare - addition
    return np.array(given)


def setup_inputs(seed: int = 0) -> dict:
    keys = jax.random.split(jax.random.key(seed), 6)
    estimate = jnp.clip(jnp.exp(math.log(2.0) - 1.3862944 * jax.random.uniform(keys[0], (NBXY, NZ, R), jnp.float32) ** shard_levels(keys[0], (NBXY, NZ, R), ((0, 16), (1, 2)), -0.2, 0.2)), 0.5, 2.0)
    views = jnp.clip(jnp.exp(math.log(4.0) - 2.7725887 * jax.random.uniform(keys[1], (NBXY, VIEWS, NZ, R), jnp.float32) ** shard_levels(keys[1], (NBXY, VIEWS, NZ, R), ((0, 16), (2, 2)), -0.2, 0.2)), 0.25, 4.0).astype(jnp.bfloat16)
    owners_keys = jax.random.split(jax.random.fold_in(keys[2], 1), NBXY // BXY_DEV)
    owners_turns = jax.random.permutation(jax.random.fold_in(keys[2], 3), NBXY // BXY_DEV)
    owners = jax.vmap(lambda own, number: routed_block(jax.random.fold_in(keys[2], 2), own, number, BXY_DEV, N_JOIN, VIEWS, CAP, 2))(owners_keys, owners_turns).reshape((NBXY, VIEWS))
    local_blocks = draw_local_blocks(jax.random.fold_in(keys[5], 71), 0)
    psf = jnp.clip(jnp.exp(jax.random.uniform(keys[4], (VIEWS, TAPS), jnp.float32, math.log(0.05), math.log(1.0))), 0.05, 1.0)
    return {"estimate": estimate, "views": views, "owners": owners, "local_blocks": local_blocks, "psf": psf}


def along_axis(field, kernel):
    padded = jnp.pad(field, ((0, 0), (H, H), (0, 0)))
    total = jnp.zeros(field.shape, jnp.float32)
    for tap in range(TAPS):
        total = total + kernel[tap] * padded[:, tap:tap + NZ, :]
    return total


def reference(estimate, views, owners, local_blocks, psf):
    normed = psf / jnp.sum(psf, axis=1, keepdims=True)
    kernel = lax.optimization_barrier(normed.astype(jnp.bfloat16)).astype(jnp.float32)
    footprint = (owners * BXY_DEV + local_blocks).astype(jnp.int32)
    counts = jnp.zeros((NBXY,), jnp.float32).at[footprint.reshape(-1)].add(1.0)
    current = estimate
    for sweep in range(ITERS):
        rounded = lax.optimization_barrier(current.astype(jnp.bfloat16)).astype(jnp.float32)
        summed = jnp.zeros(current.shape, jnp.float32)
        for which in range(VIEWS):
            seen_est = rounded[footprint[:, which]]
            blurred = along_axis(seen_est, kernel[which])
            quotient = views[:, which].astype(jnp.float32) / blurred
            quotient = lax.optimization_barrier(quotient.astype(jnp.bfloat16)).astype(jnp.float32)
            correction = along_axis(quotient, kernel[which, ::-1])
            summed = summed.at[footprint[:, which]].add(correction)
        factor = jnp.where((counts > 0)[:, None, None], summed / jnp.maximum(counts, 1.0)[:, None, None], 1.0)
        current = current * factor
    return current
```

```python
import functools

import jax
import jax.numpy as jnp
from jax import lax
from jax.experimental import pallas as pl
from jax.experimental.pallas import tpu as pltpu
from jax.sharding import PartitionSpec as P

H = 16
CAP = 3
ITERS = 2
GROUP = 4
EST_HALO = 2 * ITERS * H
VIEW_HALO = EST_HALO - H

SMEM = pl.BlockSpec(memory_space=pltpu.SMEM)
VMEM = pl.BlockSpec(memory_space=pltpu.VMEM)
ANY = pl.BlockSpec(memory_space=pl.ANY)


def pack_kernel(cap, owners, blocks_of, views, out, table, seen, sems):
    blocks, nviews = views.shape[0], views.shape[1]
    peers = out.shape[0] // cap

    @pl.loop(0, peers)
    def _(peer):
        seen[peer] = 0

    @pl.loop(0, peers * cap)
    def _(slot):
        table[slot] = -1

    copies = []
    for i in range(blocks):
        for v in range(nviews):
            owner = owners[i, v]
            order = seen[owner]
            seen[owner] = order + 1
            slot = owner * cap + order
            table[slot] = blocks_of[i, v] * nviews + v
            copy = pltpu.make_async_copy(views.at[i, v], out.at[slot], sems.at[i * nviews + v])
            copy.start()
            copies.append(copy)
    for copy in copies:
        copy.wait()


def pack(views, owners, blocks_of, peers):
    blocks, nviews, depth, lat = views.shape
    return pl.pallas_call(
        functools.partial(pack_kernel, CAP),
        out_shape=(
            jax.ShapeDtypeStruct((peers * CAP, depth, lat), views.dtype),
            jax.ShapeDtypeStruct((peers * CAP,), jnp.int32),
        ),
        in_specs=[SMEM, SMEM, ANY],
        out_specs=(ANY, SMEM),
        scratch_shapes=[
            pltpu.SMEM((peers,), jnp.int32),
            pltpu.SemaphoreType.DMA((blocks * nviews,)),
        ],
        name="pack",
    )(owners, blocks_of, views)


def toeplitz_kernel(taps, kernel, forward, mirror):
    nviews, frame = forward.shape[0], forward.shape[1]
    row = lax.broadcasted_iota(jnp.int32, (frame, frame), 0)
    column = lax.broadcasted_iota(jnp.int32, (frame, frame), 1)
    for ref, tap_at in ((forward, column - row + H), (mirror, row - column + H)):

        @pl.loop(0, nviews)
        def _(v):
            def put(t, total):
                return jnp.where(tap_at == t, kernel[v, t], total)

            total = lax.fori_loop(0, taps, put, jnp.zeros((frame, frame), jnp.float32))
            ref[v] = total.astype(ref.dtype)


def toeplitz(kernel, frame):
    nviews, taps = kernel.shape
    shape = jax.ShapeDtypeStruct((nviews, frame, frame), jnp.bfloat16)
    return pl.pallas_call(
        functools.partial(toeplitz_kernel, taps),
        out_shape=(shape, shape),
        in_specs=[SMEM],
        out_specs=(VMEM, VMEM),
        name="toeplitz",
    )(kernel.astype(jnp.float32))


def deconvolve_kernel(
    pieces, guard, codes, offsets, *refs
):
    sources = refs[: len(pieces)]
    est, forward, mirror, out = refs[len(pieces) : len(pieces) + 4]
    held, recip, current, total, slot_of, code_of, counts, starts, sems = refs[len(pieces) + 4 :]
    nviews, frame = forward.shape[0], forward.shape[1]
    blocks, depth, lat = out.shape
    slots = codes.shape[0]
    blank = held.shape[0] - 1

    for b in range(blocks):
        counts[b] = 0

    @pl.loop(0, slots)
    def _(slot):
        code = codes[slot]

        @pl.when(code >= 0)
        def _():
            b = code // nviews
            counts[b] = counts[b] + 1
            for which, (source, rows) in enumerate(zip(sources, pieces)):
                at = pl.multiple_of(offsets[which], H)
                pltpu.make_async_copy(
                    source.at[slot], held.at[slot, pl.ds(at, rows)], sems.at[slot, which]
                ).start()

    start = jnp.int32(0)
    for b in range(blocks):
        starts[b] = start
        start = start + (counts[b] + (GROUP - 1)) // GROUP * GROUP
    starts[blocks] = start

    @pl.loop(0, slot_of.shape[0])
    def _(p):
        slot_of[p] = blank
        code_of[p] = 0

    @pl.loop(0, slots)
    def _(slot):
        code = codes[slot]

        @pl.when(code >= 0)
        def _():
            b = code // nviews
            p = starts[b]
            starts[b] = p + 1
            slot_of[p] = slot
            code_of[p] = code - b * nviews

    start = jnp.int32(0)
    for b in range(blocks):
        starts[b] = start
        start = start + (counts[b] + (GROUP - 1)) // GROUP * GROUP

    held[blank] = jnp.zeros(held.shape[1:], held.dtype)
    covered = sum(pieces)
    if covered < frame:
        edge = frame - covered
        sides = 1 if len(pieces) == 2 else 2
        for side in range(sides):
            at = pl.multiple_of(offsets[len(pieces) + side], H)

            @pl.loop(0, slots)
            def _(slot):
                held[slot, pl.ds(at, edge // sides)] = jnp.zeros((edge // sides, lat), held.dtype)

    current[...] = est[...]
    for sweep in range(ITERS):
        for b in range(blocks):

            @pl.when(counts[b] > 0)
            def _():
                rounded = current[b].astype(jnp.bfloat16)

                @pl.loop(0, nviews)
                def _(v):
                    blurred = jnp.dot(forward[v], rounded, preferred_element_type=jnp.float32)
                    inverse = 1.0 / blurred
                    if guard:
                        inverse = jnp.where(blurred > 0, inverse, 0.0)
                    recip[b, v] = inverse

        if sweep == 0:

            @pl.loop(0, slots)
            def _(slot):
                @pl.when(codes[slot] >= 0)
                def _():
                    for which, (source, rows) in enumerate(zip(sources, pieces)):
                        at = pl.multiple_of(offsets[which], H)
                        pltpu.make_async_copy(
                            source.at[slot], held.at[slot, pl.ds(at, rows)], sems.at[slot, which]
                        ).wait()

        for b in range(blocks):

            @pl.when(counts[b] > 0)
            def _():
                total[...] = jnp.zeros_like(total)

                @pl.loop(0, (counts[b] + (GROUP - 1)) // GROUP)
                def _(group):
                    first = starts[b] + group * GROUP
                    gained = None
                    for member in range(GROUP):
                        v = code_of[first + member]
                        quotient = (
                            held[slot_of[first + member]].astype(jnp.float32) * recip[b, v]
                        ).astype(jnp.bfloat16)
                        part = jnp.dot(mirror[v], quotient, preferred_element_type=jnp.float32)
                        gained = part if gained is None else gained + part
                    total[...] += gained

                current[b] = current[b] * (total[...] / counts[b].astype(jnp.float32))

    own = pl.multiple_of(offsets[0], H)
    out[...] = current[:, pl.ds(own, depth)]


def deconvolve(codes, offsets, sources, est, forward, mirror, depth, guard):
    blocks, frame, lat = est.shape
    nviews = forward.shape[0]
    slots = codes.shape[0]
    pieces = tuple(source.shape[1] for source in sources)
    listed = slots + blocks * GROUP
    return pl.pallas_call(
        functools.partial(deconvolve_kernel, pieces, guard),
        out_shape=jax.ShapeDtypeStruct((blocks, depth, lat), jnp.float32),
        in_specs=[SMEM, SMEM] + [ANY] * len(sources) + [VMEM, VMEM, VMEM],
        out_specs=VMEM,
        scratch_shapes=[
            pltpu.VMEM((slots + 1, frame, lat), jnp.bfloat16),
            pltpu.VMEM((blocks, nviews, frame, lat), jnp.float32),
            pltpu.VMEM((blocks, frame, lat), jnp.float32),
            pltpu.VMEM((frame, lat), jnp.float32),
            pltpu.SMEM((listed,), jnp.int32),
            pltpu.SMEM((listed,), jnp.int32),
            pltpu.SMEM((blocks,), jnp.int32),
            pltpu.SMEM((blocks + 1,), jnp.int32),
            pltpu.SemaphoreType.DMA((slots, len(sources))),
        ],
        compiler_params=pltpu.CompilerParams(vmem_limit_bytes=40 * 1024 * 1024),
        name="deconvolve",
    )(codes, offsets, *sources, est, forward, mirror)


def halos(block, dim, width):
    count = lax.axis_size("view")
    depth = block.shape[dim]
    if count == 1:
        return ()
    if count == 2:
        start = jnp.where(lax.axis_index("view") == 0, depth - width, 0)
        sent = lax.dynamic_slice_in_dim(block, start, width, axis=dim)
        return (lax.ppermute(sent, "view", [(0, 1), (1, 0)]),)
    forward = [(i, i + 1) for i in range(count - 1)]
    backward = [(target, source) for source, target in forward]
    low = lax.ppermute(lax.slice_in_dim(block, depth - width, depth, axis=dim), "view", forward)
    high = lax.ppermute(lax.slice_in_dim(block, 0, width, axis=dim), "view", backward)
    return (low, high)


def framed(block, sides, dim):
    if not sides:
        return block
    if len(sides) == 2:
        return jnp.concatenate([sides[0], block, sides[1]], axis=dim)
    (side,) = sides
    return jnp.where(
        lax.axis_index("view") == 0,
        jnp.concatenate([block, side], axis=dim),
        jnp.concatenate([side, block], axis=dim),
    )


def frame_offsets(depth):
    count = lax.axis_size("view")
    empty = EST_HALO - VIEW_HALO
    if count == 1:
        return jnp.zeros((1,), jnp.int32)
    if count == 2:
        first = jnp.array([0, depth, depth + VIEW_HALO], jnp.int32)
        second = jnp.array([EST_HALO, empty, 0], jnp.int32)
        return jnp.where(lax.axis_index("view") == 0, first, second)
    return jnp.array(
        [EST_HALO, empty, EST_HALO + depth, 0, EST_HALO + depth + VIEW_HALO], jnp.int32
    )


def gathered_tables(table, axis):
    count = lax.axis_size(axis)
    if count & (count - 1):
        return lax.all_gather(table, axis, axis=0)
    rows = table[None]
    here = lax.axis_index(axis)
    step = 1
    while step < count:
        other = lax.ppermute(rows, axis, [(i, i ^ step) for i in range(count)])
        rows = jnp.where(
            (here & step) == 0,
            jnp.concatenate([rows, other], axis=0),
            jnp.concatenate([other, rows], axis=0),
        )
        step *= 2
    return rows


def local(estimate, views, owners, local_blocks, psf):
    blocks, depth, lat = estimate.shape
    peers = lax.axis_size("join")
    normed = psf / jnp.sum(psf, axis=1, keepdims=True)
    kernel = normed.astype(jnp.bfloat16)

    packed, table = pack(views, owners, local_blocks, peers)
    arrived = lax.all_to_all(
        packed.reshape(peers, CAP, depth, lat), "join", split_axis=0, concat_axis=0, tiled=True
    ).reshape(peers * CAP, depth, lat)

    tables = gathered_tables(table, "join").reshape(peers, peers, CAP)
    codes = lax.dynamic_index_in_dim(tables, lax.axis_index("join"), axis=1, keepdims=False)
    est = framed(estimate, halos(estimate, 1, EST_HALO), 1)
    forward, mirror = toeplitz(kernel, est.shape[1])

    sides = halos(arrived, 1, VIEW_HALO)
    return deconvolve(
        codes.reshape(-1),
        frame_offsets(depth),
        (arrived,) + sides,
        est,
        forward,
        mirror,
        depth,
        lax.axis_size("view") > 2,
    )


def solution(mesh):
    in_specs = (
        P("join", "view", None),
        P("join", None, "view", None),
        P("join", None),
        P("join", None),
        P(),
    )
    out_specs = P("join", "view", None)
    return jax.shard_map(local, mesh=mesh, in_specs=in_specs, out_specs=out_specs, check_vma=False)
```

```python
import functools

import jax
import jax.numpy as jnp
from jax import lax
from jax.experimental import pallas as pl
from jax.experimental.pallas import tpu as pltpu
from jax.sharding import PartitionSpec as P

H = 16
CAP = 3
ITERS = 2
GROUP = 4
EST_HALO = 2 * ITERS * H
VIEW_HALO = EST_HALO - H

SMEM = pl.BlockSpec(memory_space=pltpu.SMEM)
VMEM = pl.BlockSpec(memory_space=pltpu.VMEM)
ANY = pl.BlockSpec(memory_space=pl.ANY)


def pack_kernel(cap, owners, blocks_of, views, out, table, seen, staged, in_sems, out_sems):
    blocks, nviews = views.shape[0], views.shape[1]
    peers = out.shape[0] // cap

    pairs = [(i, v) for i in range(blocks) for v in range(nviews)]
    loads = [
        pltpu.make_async_copy(views.at[i, v], staged.at[i, v], in_sems.at[i, v]) for i, v in pairs
    ]
    for load in loads:
        load.start()

    @pl.loop(0, peers)
    def _(peer):
        seen[peer] = 0

    @pl.loop(0, peers * cap)
    def _(slot):
        table[slot] = -1

    stores = []
    for (i, v), load in zip(pairs, loads):
        owner = owners[i, v]
        order = seen[owner]
        seen[owner] = order + 1
        slot = owner * cap + order
        table[slot] = blocks_of[i, v] * nviews + v
        load.wait()
        store = pltpu.make_async_copy(staged.at[i, v], out.at[slot], out_sems.at[i, v])
        store.start()
        stores.append(store)
    for store in stores:
        store.wait()


def pack(views, owners, blocks_of, peers):
    blocks, nviews, depth, lat = views.shape
    return pl.pallas_call(
        functools.partial(pack_kernel, CAP),
        out_shape=(
            jax.ShapeDtypeStruct((peers * CAP, depth, lat), views.dtype),
            jax.ShapeDtypeStruct((peers * CAP,), jnp.int32),
        ),
        in_specs=[SMEM, SMEM, ANY],
        out_specs=(ANY, SMEM),
        scratch_shapes=[
            pltpu.SMEM((peers,), jnp.int32),
            pltpu.VMEM(views.shape, views.dtype),
            pltpu.SemaphoreType.DMA((blocks, nviews)),
            pltpu.SemaphoreType.DMA((blocks, nviews)),
        ],
        name="pack",
    )(owners, blocks_of, views)


def toeplitz_kernel(taps, kernel, forward, mirror):
    nviews, frame = forward.shape[0], forward.shape[1]
    row = lax.broadcasted_iota(jnp.int32, (frame, frame), 0)
    column = lax.broadcasted_iota(jnp.int32, (frame, frame), 1)
    for ref, tap_at in ((forward, column - row + H), (mirror, row - column + H)):

        @pl.loop(0, nviews)
        def _(v):
            def put(t, total):
                return jnp.where(tap_at == t, kernel[v, t], total)

            total = lax.fori_loop(0, taps, put, jnp.zeros((frame, frame), jnp.float32))
            ref[v] = total.astype(ref.dtype)


def toeplitz(kernel, frame):
    nviews, taps = kernel.shape
    shape = jax.ShapeDtypeStruct((nviews, frame, frame), jnp.bfloat16)
    return pl.pallas_call(
        functools.partial(toeplitz_kernel, taps),
        out_shape=(shape, shape),
        in_specs=[SMEM],
        out_specs=(VMEM, VMEM),
        name="toeplitz",
    )(kernel.astype(jnp.float32))


def deconvolve_kernel(
    pieces, guard, codes, offsets, *refs
):
    sources = refs[: len(pieces)]
    est, forward, mirror, out = refs[len(pieces) : len(pieces) + 4]
    held, recip, current, total, slot_of, code_of, counts, starts, sems = refs[len(pieces) + 4 :]
    nviews, frame = forward.shape[0], forward.shape[1]
    blocks, depth, lat = out.shape
    slots = codes.shape[0]
    blank = held.shape[0] - 1

    for b in range(blocks):
        counts[b] = 0

    @pl.loop(0, slots)
    def _(slot):
        code = codes[slot]

        @pl.when(code >= 0)
        def _():
            b = code // nviews
            counts[b] = counts[b] + 1
            for which, (source, rows) in enumerate(zip(sources, pieces)):
                at = pl.multiple_of(offsets[which], H)
                pltpu.make_async_copy(
                    source.at[slot], held.at[slot, pl.ds(at, rows)], sems.at[slot, which]
                ).start()

    start = jnp.int32(0)
    for b in range(blocks):
        starts[b] = start
        start = start + (counts[b] + (GROUP - 1)) // GROUP * GROUP
    starts[blocks] = start

    @pl.loop(0, slot_of.shape[0])
    def _(p):
        slot_of[p] = blank
        code_of[p] = 0

    @pl.loop(0, slots)
    def _(slot):
        code = codes[slot]

        @pl.when(code >= 0)
        def _():
            b = code // nviews
            p = starts[b]
            starts[b] = p + 1
            slot_of[p] = slot
            code_of[p] = code - b * nviews

    start = jnp.int32(0)
    for b in range(blocks):
        starts[b] = start
        start = start + (counts[b] + (GROUP - 1)) // GROUP * GROUP

    held[blank] = jnp.zeros(held.shape[1:], held.dtype)
    covered = sum(pieces)
    if covered < frame:
        edge = frame - covered
        sides = 1 if len(pieces) == 2 else 2
        for side in range(sides):
            at = pl.multiple_of(offsets[len(pieces) + side], H)

            @pl.loop(0, slots)
            def _(slot):
                held[slot, pl.ds(at, edge // sides)] = jnp.zeros((edge // sides, lat), held.dtype)

    current[...] = est[...]
    for sweep in range(ITERS):
        for b in range(blocks):

            @pl.when(counts[b] > 0)
            def _():
                rounded = current[b].astype(jnp.bfloat16)

                @pl.loop(0, nviews)
                def _(v):
                    blurred = jnp.dot(forward[v], rounded, preferred_element_type=jnp.float32)
                    inverse = 1.0 / blurred
                    if guard:
                        inverse = jnp.where(blurred > 0, inverse, 0.0)
                    recip[b, v] = inverse

        if sweep == 0:

            @pl.loop(0, slots)
            def _(slot):
                @pl.when(codes[slot] >= 0)
                def _():
                    for which, (source, rows) in enumerate(zip(sources, pieces)):
                        at = pl.multiple_of(offsets[which], H)
                        pltpu.make_async_copy(
                            source.at[slot], held.at[slot, pl.ds(at, rows)], sems.at[slot, which]
                        ).wait()

        for b in range(blocks):

            @pl.when(counts[b] > 0)
            def _():
                total[...] = jnp.zeros_like(total)

                @pl.loop(0, (counts[b] + (GROUP - 1)) // GROUP)
                def _(group):
                    first = starts[b] + group * GROUP
                    gained = None
                    for member in range(GROUP):
                        v = code_of[first + member]
                        quotient = (
                            held[slot_of[first + member]].astype(jnp.float32) * recip[b, v]
                        ).astype(jnp.bfloat16)
                        part = jnp.dot(mirror[v], quotient, preferred_element_type=jnp.float32)
                        gained = part if gained is None else gained + part
                    total[...] += gained

                current[b] = current[b] * (total[...] / counts[b].astype(jnp.float32))

    own = pl.multiple_of(offsets[0], H)
    out[...] = current[:, pl.ds(own, depth)]


def deconvolve(codes, offsets, sources, est, forward, mirror, depth, guard):
    blocks, frame, lat = est.shape
    nviews = forward.shape[0]
    slots = codes.shape[0]
    pieces = tuple(source.shape[1] for source in sources)
    listed = slots + blocks * GROUP
    return pl.pallas_call(
        functools.partial(deconvolve_kernel, pieces, guard),
        out_shape=jax.ShapeDtypeStruct((blocks, depth, lat), jnp.float32),
        in_specs=[SMEM, SMEM] + [ANY] * len(sources) + [VMEM, VMEM, VMEM],
        out_specs=VMEM,
        scratch_shapes=[
            pltpu.VMEM((slots + 1, frame, lat), jnp.bfloat16),
            pltpu.VMEM((blocks, nviews, frame, lat), jnp.float32),
            pltpu.VMEM((blocks, frame, lat), jnp.float32),
            pltpu.VMEM((frame, lat), jnp.float32),
            pltpu.SMEM((listed,), jnp.int32),
            pltpu.SMEM((listed,), jnp.int32),
            pltpu.SMEM((blocks,), jnp.int32),
            pltpu.SMEM((blocks + 1,), jnp.int32),
            pltpu.SemaphoreType.DMA((slots, len(sources))),
        ],
        compiler_params=pltpu.CompilerParams(vmem_limit_bytes=40 * 1024 * 1024),
        name="deconvolve",
    )(codes, offsets, *sources, est, forward, mirror)


def halos(block, dim, width):
    count = lax.axis_size("view")
    depth = block.shape[dim]
    if count == 1:
        return ()
    if count == 2:
        start = jnp.where(lax.axis_index("view") == 0, depth - width, 0)
        sent = lax.dynamic_slice_in_dim(block, start, width, axis=dim)
        return (lax.ppermute(sent, "view", [(0, 1), (1, 0)]),)
    forward = [(i, i + 1) for i in range(count - 1)]
    backward = [(target, source) for source, target in forward]
    low = lax.ppermute(lax.slice_in_dim(block, depth - width, depth, axis=dim), "view", forward)
    high = lax.ppermute(lax.slice_in_dim(block, 0, width, axis=dim), "view", backward)
    return (low, high)


def framed(block, sides, dim):
    if not sides:
        return block
    if len(sides) == 2:
        return jnp.concatenate([sides[0], block, sides[1]], axis=dim)
    (side,) = sides
    return jnp.where(
        lax.axis_index("view") == 0,
        jnp.concatenate([block, side], axis=dim),
        jnp.concatenate([side, block], axis=dim),
    )


def frame_offsets(depth):
    count = lax.axis_size("view")
    empty = EST_HALO - VIEW_HALO
    if count == 1:
        return jnp.zeros((1,), jnp.int32)
    if count == 2:
        first = jnp.array([0, depth, depth + VIEW_HALO], jnp.int32)
        second = jnp.array([EST_HALO, empty, 0], jnp.int32)
        return jnp.where(lax.axis_index("view") == 0, first, second)
    return jnp.array(
        [EST_HALO, empty, EST_HALO + depth, 0, EST_HALO + depth + VIEW_HALO], jnp.int32
    )


def gathered_tables(table, axis):
    count = lax.axis_size(axis)
    if count & (count - 1):
        return lax.all_gather(table, axis, axis=0)
    rows = table[None]
    here = lax.axis_index(axis)
    step = 1
    while step < count:
        other = lax.ppermute(rows, axis, [(i, i ^ step) for i in range(count)])
        rows = jnp.where(
            (here & step) == 0,
            jnp.concatenate([rows, other], axis=0),
            jnp.concatenate([other, rows], axis=0),
        )
        step *= 2
    return rows


def local(estimate, views, owners, local_blocks, psf):
    blocks, depth, lat = estimate.shape
    peers = lax.axis_size("join")
    normed = psf / jnp.sum(psf, axis=1, keepdims=True)
    kernel = normed.astype(jnp.bfloat16)

    packed, table = pack(views, owners, local_blocks, peers)
    arrived = lax.all_to_all(
        packed.reshape(peers, CAP, depth, lat), "join", split_axis=0, concat_axis=0, tiled=True
    ).reshape(peers * CAP, depth, lat)

    tables = gathered_tables(table, "join").reshape(peers, peers, CAP)
    codes = lax.dynamic_index_in_dim(tables, lax.axis_index("join"), axis=1, keepdims=False)
    est = framed(estimate, halos(estimate, 1, EST_HALO), 1)
    forward, mirror = toeplitz(kernel, est.shape[1])
    arrived, codes, est, forward, mirror = lax.optimization_barrier(
        (arrived, codes, est, forward, mirror)
    )

    sides = halos(arrived, 1, VIEW_HALO)
    return deconvolve(
        codes.reshape(-1),
        frame_offsets(depth),
        (arrived,) + sides,
        est,
        forward,
        mirror,
        depth,
        lax.axis_size("view") > 2,
    )


def solution(mesh):
    in_specs = (
        P("join", "view", None),
        P("join", None, "view", None),
        P("join", None),
        P("join", None),
        P(),
    )
    out_specs = P("join", "view", None)
    return jax.shard_map(local, mesh=mesh, in_specs=in_specs, out_specs=out_specs, check_vma=False)
```

```python
import functools

import jax
import jax.numpy as jnp
from jax import lax
from jax.experimental import pallas as pl
from jax.experimental.pallas import tpu as pltpu
from jax.sharding import PartitionSpec as P

H = 16
CAP = 3
MAIN = 2
ITERS = 2
GROUP = 8
TILE = 16
EST_HALO = 2 * ITERS * H
VIEW_HALO = EST_HALO - H

SMEM = pl.BlockSpec(memory_space=pltpu.SMEM)
VMEM = pl.BlockSpec(memory_space=pltpu.VMEM)
ANY = pl.BlockSpec(memory_space=pl.ANY)


def pack_kernel(owners, blocks_of, here, views, main, *refs):
    rows, (table, seen, taken, staged, table_rows, in_sems, out_sems, table_sems) = refs[:-8], refs[-8:]
    blocks, nviews, depth, lat = views.shape
    peers, groups = seen.shape[0], len(rows)
    members = peers // groups
    pairs = [(i, v) for i in range(blocks) for v in range(nviews)]
    loads = [
        pltpu.make_async_copy(views.at[i, v], staged.at[i, v], in_sems.at[i, v]) for i, v in pairs
    ]
    for load in loads:
        load.start()

    @pl.loop(0, peers)
    def _(peer):
        seen[peer] = 0

    for group in range(groups):
        taken[group] = 0

    @pl.loop(0, peers * CAP)
    def _(slot):
        table[slot] = -1

    table[peers * CAP] = 0
    stores = []
    for (i, v), load in zip(pairs, loads):
        owner = owners[i, v]
        order = seen[owner]
        seen[owner] = order + 1
        table[owner * CAP + order] = blocks_of[i, v] * nviews + v
        away = lax.rem(owner // members + groups - here[0], groups)
        in_main = order < MAIN
        in_rows = jnp.logical_and(jnp.logical_not(in_main), taken[away] == 0)
        load.wait()

        @pl.when(in_main)
        def _():
            pltpu.make_async_copy(
                staged.at[i, v], main.at[owner * MAIN + order], out_sems.at[i, v]
            ).start()

        @pl.when(jnp.logical_not(in_main))
        def _():
            table[peers * CAP] = jnp.where(in_rows, table[peers * CAP], 1)
            for k in range(groups):

                @pl.when(jnp.logical_and(in_rows, away == k))
                def _():
                    taken[k] = 1
                    pltpu.make_async_copy(
                        staged.at[i, v], rows[k].at[0, pl.ds(0, depth)], out_sems.at[i, v]
                    ).start()

        stores.append((i, v, jnp.logical_or(in_main, in_rows)))

    lane = lax.broadcasted_iota(jnp.int32, (TILE, lat), 1)
    row = jnp.full((TILE, lat), -1, jnp.int32)
    for slot in range(peers * CAP + 1):
        row = jnp.where(lane == slot, table[slot], row)
    table_rows[...] = row.astype(jnp.float32).astype(table_rows.dtype)
    table_stores = [
        pltpu.make_async_copy(table_rows, rows[k].at[0, pl.ds(depth, TILE)], table_sems.at[k])
        for k in range(groups)
    ]
    for store in table_stores:
        store.start()
    for i, v, stored in stores:

        @pl.when(stored)
        def _():
            pltpu.make_async_copy(staged.at[i, v], main.at[0], out_sems.at[i, v]).wait()

    for store in table_stores:
        store.wait()


def pack(views, owners, blocks_of, here, peers, groups):
    blocks, nviews, depth, lat = views.shape
    assert peers * CAP < lat
    return pl.pallas_call(
        pack_kernel,
        out_shape=(jax.ShapeDtypeStruct((peers * MAIN, depth, lat), views.dtype),)
        + (jax.ShapeDtypeStruct((1, depth + TILE, lat), views.dtype),) * groups,
        in_specs=[SMEM, SMEM, SMEM, ANY],
        out_specs=(ANY,) * (1 + groups),
        scratch_shapes=[
            pltpu.SMEM((peers * CAP + 1,), jnp.int32),
            pltpu.SMEM((peers,), jnp.int32),
            pltpu.SMEM((groups,), jnp.int32),
            pltpu.VMEM(views.shape, views.dtype),
            pltpu.VMEM((TILE, lat), views.dtype),
            pltpu.SemaphoreType.DMA((blocks, nviews)),
            pltpu.SemaphoreType.DMA((blocks, nviews)),
            pltpu.SemaphoreType.DMA((groups,)),
        ],
        name="pack",
    )(owners, blocks_of, here, views)


def all_thirds_kernel(owners, views, out, seen, staged, sems):
    blocks, nviews = views.shape[0], views.shape[1]

    @pl.loop(0, out.shape[0])
    def _(peer):
        seen[peer] = 0

    for i in range(blocks):
        for v in range(nviews):
            owner = owners[i, v]
            order = seen[owner]
            seen[owner] = order + 1

            @pl.when(order >= MAIN)
            def _():
                load = pltpu.make_async_copy(views.at[i, v], staged, sems.at[0])
                load.start()
                load.wait()
                store = pltpu.make_async_copy(staged, out.at[owner], sems.at[1])
                store.start()
                store.wait()


def pack_all_thirds(views, owners, peers):
    depth, lat = views.shape[2:]
    return pl.pallas_call(
        all_thirds_kernel,
        out_shape=jax.ShapeDtypeStruct((peers, depth, lat), views.dtype),
        in_specs=[SMEM, ANY],
        out_specs=ANY,
        scratch_shapes=[
            pltpu.SMEM((peers,), jnp.int32),
            pltpu.VMEM((depth, lat), views.dtype),
            pltpu.SemaphoreType.DMA((2,)),
        ],
        name="all_thirds",
    )(owners, views)


def group_count(peers):
    members = 1
    while peers % (2 * members) == 0 and members * members < peers:
        members *= 2
    return peers // members


def along_groups(rows):
    peers = lax.axis_size("join")
    members = peers // len(rows)
    line = [rows[0]]
    for k in range(1, len(rows)):
        line.append(
            lax.ppermute(rows[k], "join", [(i, (i + k * members) % peers) for i in range(peers)])
        )
    return line


def among_members(line):
    peers = lax.axis_size("join")
    members = peers // len(line)
    line = jnp.concatenate(line, axis=0)
    parts = [line]
    for m in range(1, members):
        parts.append(lax.ppermute(line, "join", [(i, i ^ m) for i in range(peers)]))
    return parts


def sources_of_parts(groups):
    peers = lax.axis_size("join")
    members = peers // groups
    here = lax.axis_index("join")
    at = jnp.arange(peers, dtype=jnp.int32)
    group = lax.rem(here // members + groups - lax.rem(at, groups), groups)
    return group * members + jnp.bitwise_xor(lax.rem(here, members), at // groups)


def ends_kernel(start, *refs):
    blocks, out, sems = refs[:-2], refs[-2], refs[-1]
    width = out.shape[1]
    copies, first = [], 0
    for k, block in enumerate(blocks):
        number = block.shape[0]
        copies.append(
            pltpu.make_async_copy(
                block.at[:, pl.ds(pl.multiple_of(start[0], TILE), width)],
                out.at[pl.ds(first, number)],
                sems.at[k],
            )
        )
        first += number
    for copy in copies:
        copy.start()
    for copy in copies:
        copy.wait()


def ends(blocks, start, width):
    if len(blocks) == 1:
        return lax.dynamic_slice_in_dim(blocks[0], start, width, axis=1)
    number = sum(block.shape[0] for block in blocks)
    return pl.pallas_call(
        ends_kernel,
        out_shape=jax.ShapeDtypeStruct((number, width, blocks[0].shape[2]), blocks[0].dtype),
        in_specs=[SMEM] + [ANY] * len(blocks),
        out_specs=ANY,
        scratch_shapes=[pltpu.SemaphoreType.DMA((len(blocks),))],
        name="ends",
    )(jnp.asarray(start, jnp.int32)[None], *blocks)


def halos(blocks, depth, width):
    count = lax.axis_size("view")
    if count == 1:
        return []
    if count == 2:
        sent = ends(blocks, jnp.where(lax.axis_index("view") == 0, depth - width, 0), width)
        return [lax.ppermute(sent, "view", [(0, 1), (1, 0)])]
    forward = [(i, i + 1) for i in range(count - 1)]
    backward = [(target, source) for source, target in forward]
    low = lax.ppermute(ends(blocks, depth - width, width), "view", forward)
    high = lax.ppermute(ends(blocks, 0, width), "view", backward)
    return [low, high]


def framed(block, sides, dim):
    if not sides:
        return block
    if len(sides) == 2:
        return jnp.concatenate([sides[0], block, sides[1]], axis=dim)
    (side,) = sides
    return jnp.where(
        lax.axis_index("view") == 0,
        jnp.concatenate([block, side], axis=dim),
        jnp.concatenate([side, block], axis=dim),
    )


def low_rows():
    count = lax.axis_size("view")
    if count == 2:
        return jnp.where(lax.axis_index("view") == 0, 0, H).astype(jnp.int32)
    return jnp.int32(0 if count == 1 else H)


def halo_rows(sweep):
    return VIEW_HALO - 2 * H * sweep


def piece_starts(depth, sweep):
    count = lax.axis_size("view")
    width = halo_rows(sweep)
    if count == 1:
        return [jnp.int32(0)]
    if count == 2:
        first = lax.axis_index("view") == 0
        return [jnp.where(first, 0, width), jnp.where(first, depth, 0)]
    return [jnp.int32(width), jnp.int32(0), jnp.int32(width + depth)]


def bands_kernel(shapes, shifts, taps_rows, *refs):
    width = taps_rows.shape[-1]
    nviews = taps_rows.shape[1]

    def band(which, v, shift, rows):
        spread = jnp.broadcast_to(taps_rows[which, v : v + 1, :], (rows, width))
        return pltpu.roll(pltpu.roll(spread, 0, 1, stride=1, stride_axis=0), shift, 1)

    at = 0
    for sweep, pieces in enumerate(shapes):
        forward, mirror = refs[2 * sweep], refs[2 * sweep + 1]
        columns, outs = forward.shape[2], mirror.shape[1]
        lane = lax.broadcasted_iota(jnp.int32, (outs, width), 1)
        for v in range(nviews):
            total = jnp.zeros((outs, width), jnp.float32)
            first = 0
            for piece, rows in enumerate(pieces):
                part = band(0, v, shifts[at + 2 * piece], rows)
                forward[v, first : first + rows] = part[:, :columns].astype(forward.dtype)
                inside = jnp.logical_and(lane >= first, lane < first + rows)
                total = jnp.where(inside, band(1, v, shifts[at + 2 * piece + 1], outs), total)
                first += rows
            mirror[v] = total[:, :first].astype(mirror.dtype)
        at += 2 * len(pieces)


def bands(kernel, depth, sides):
    nviews, taps = kernel.shape
    low = low_rows()
    frame = depth + sides * EST_HALO
    width = -(-(frame + 4 * H) // 128) * 128
    shapes, shifts, outs = [], [], []
    for sweep in range(ITERS):
        pieces = (depth,) + (halo_rows(sweep),) * sides
        first = 0
        for rows, start in zip(pieces, piece_starts(depth, sweep)):
            shifts.append(lax.rem(start + low - H + width, width))
            shifts.append(lax.rem(first - start + low - H + width, width))
            first += rows
        shapes.append(pieces)
        rows_in = frame - 2 * sides * H * sweep
        outs.append(jax.ShapeDtypeStruct((nviews, first, rows_in), jnp.bfloat16))
        outs.append(jax.ShapeDtypeStruct((nviews, rows_in - 2 * sides * H, first), jnp.bfloat16))
    rows = jnp.stack([kernel, kernel[:, ::-1]]).astype(jnp.float32)
    rows = jnp.pad(rows, ((0, 0), (0, 0), (0, width - taps)))
    return pl.pallas_call(
        functools.partial(bands_kernel, shapes),
        out_shape=outs,
        in_specs=[SMEM, VMEM],
        out_specs=[VMEM] * len(outs),
        name="bands",
    )(jnp.stack(shifts).astype(jnp.int32), rows)


def plan_kernel(nviews, blocks, here, source, *refs):
    parts, refs = refs[:-11], refs[-11:]
    main_slot, main_code, third_slot, third_source, third_code, numbers, any_crowded = refs[:7]
    tables, rows, scalars, sems = refs[7:]
    per_part, depth, lat = parts[0].shape
    depth -= TILE
    peers = source.shape[0]
    blank = blocks * nviews
    loads = [
        pltpu.make_async_copy(
            part.at[:, pl.ds(depth, TILE)], tables.at[pl.ds(j * per_part, per_part)], sems.at[j]
        )
        for j, part in enumerate(parts)
    ]
    for load in loads:
        load.start()
    for b in range(blocks):
        numbers[2 + b] = 0
    for load in loads:
        load.wait()
    at = lax.broadcasted_iota(jnp.int32, (peers, lat), 0)
    together = jnp.zeros((peers, lat), jnp.float32)
    for t in range(peers):
        row = jnp.broadcast_to(tables[t, :1].astype(jnp.float32), (peers, lat))
        together = jnp.where(at == t, row, together)
    rows[...] = together.astype(jnp.int32)
    copy = pltpu.make_async_copy(rows, scalars, sems.at[len(parts)])
    copy.start()
    copy.wait()

    def enlist(t, carry):
        in_main, in_third, crowded = carry
        for order in range(CAP):
            code = scalars[t, here[0] * CAP + order]
            valid = code >= 0

            @pl.when(valid)
            def _():
                b = code // nviews
                numbers[2 + b] = numbers[2 + b] + 1
                if order < MAIN:
                    main_slot[in_main] = source[t] * MAIN + order
                    main_code[in_main] = code
                else:
                    third_slot[in_third] = t
                    third_source[in_third] = source[t]
                    third_code[in_third] = code

            if order < MAIN:
                in_main = in_main + valid.astype(jnp.int32)
            else:
                in_third = in_third + valid.astype(jnp.int32)
        return in_main, in_third, jnp.maximum(crowded, scalars[t, peers * CAP])

    zero = jnp.int32(0)
    in_main, in_third, crowded = lax.fori_loop(0, peers, enlist, (zero, zero, zero))
    numbers[0] = in_main
    numbers[1] = in_third
    any_crowded[0] = crowded
    for more in range(GROUP - 1):
        main_slot[in_main + more] = main_slot[0]
        main_code[in_main + more] = blank
        third_slot[in_third + more] = third_slot[0]
        third_source[in_third + more] = third_source[0]
        third_code[in_third + more] = blank


def plan(parts, source, here, blocks, nviews):
    peers = source.shape[0]
    lat = parts[0].shape[-1]
    listed = jax.ShapeDtypeStruct((peers * MAIN + GROUP,), jnp.int32)
    thirds = jax.ShapeDtypeStruct((peers + GROUP,), jnp.int32)
    return pl.pallas_call(
        functools.partial(plan_kernel, nviews, blocks),
        out_shape=(listed,) * 2
        + (thirds,) * 3
        + (jax.ShapeDtypeStruct((2 + blocks,), jnp.int32), jax.ShapeDtypeStruct((1,), jnp.int32)),
        in_specs=[SMEM] * 2 + [ANY] * len(parts),
        out_specs=(SMEM,) * 7,
        scratch_shapes=[
            pltpu.VMEM((peers, TILE, lat), parts[0].dtype),
            pltpu.VMEM((peers, lat), jnp.int32),
            pltpu.SMEM((peers, lat), jnp.int32),
            pltpu.SemaphoreType.DMA((len(parts) + 1,)),
        ],
        name="plan",
    )(here[None], source, *parts)


def deconvolve_kernel(nparts, sides, guard, low_ref, *refs):
    main_slot, main_code, third_slot, third_code, numbers = refs[:5]
    main, refs = refs[5], refs[6:]
    parts, refs = refs[:nparts], refs[nparts:]
    main_halo, third_halo, refs = refs[:sides], refs[sides : 2 * sides], refs[2 * sides :]
    est, refs = refs[0], refs[1:]
    bands_of, refs = refs[: 2 * ITERS], refs[2 * ITERS :]
    out, held, recip, following, total, result, sems = refs
    blocks, depth, lat = out.shape
    nviews = bands_of[0].shape[0]
    per_part = parts[0].shape[0]
    low = pl.multiple_of(low_ref[0], H)
    counts = [numbers[2 + b] for b in range(blocks)]
    recip[blocks * nviews] = jnp.zeros(recip.shape[1:], recip.dtype)

    @pl.loop(0, numbers[1])
    def _(p):
        slot = third_slot[p]
        for j, part in enumerate(parts):

            @pl.when(jnp.logical_and(slot >= j * per_part, slot < (j + 1) * per_part))
            def _():
                held[p] = part[slot - j * per_part, :depth]

    stores = []
    for sweep in range(ITERS):
        current = est if sweep == 0 else following
        forward, mirror = bands_of[2 * sweep], bands_of[2 * sweep + 1]
        next_rows, view_rows = mirror.shape[1], mirror.shape[2]
        side_rows = halo_rows(sweep)
        next_at = pl.multiple_of(2 * low, 2 * H)
        halo_at = [pl.multiple_of(2 * sweep * low, 2 * H), 0]
        for b in range(blocks):

            @pl.when(counts[b] > 0)
            def _():
                rounded = current[b].astype(jnp.bfloat16)
                for v in range(nviews):
                    blurred = jnp.dot(forward[v], rounded, preferred_element_type=jnp.float32)
                    inverse = 1.0 / blurred
                    if guard:
                        inverse = jnp.where(blurred > 0, inverse, 0.0)
                    recip[b * nviews + v, :view_rows] = inverse

        total[:, :next_rows] = jnp.zeros((blocks + 1, next_rows, lat), jnp.float32)

        def add(number, held_at, halo, slot_at, code_at):
            @pl.loop(0, (number + (GROUP - 1)) // GROUP)
            def _(group):
                gained = []
                for member in range(GROUP):
                    p = group * GROUP + member
                    code = code_at[p]
                    b = code // nviews
                    pieces = [held_at(p).astype(jnp.float32) * recip[code, :depth]]
                    for side, ref in enumerate(halo):
                        first = depth + side * side_rows
                        rows = ref[slot_at[p], pl.ds(halo_at[side], side_rows)]
                        pieces.append(
                            rows.astype(jnp.float32) * recip[code, first : first + side_rows]
                        )
                    quotient = jnp.concatenate([q.astype(jnp.bfloat16) for q in pieces], axis=0)
                    part = jnp.dot(
                        mirror[code - b * nviews], quotient, preferred_element_type=jnp.float32
                    )
                    gained.append((b, part))
                for b, part in gained:
                    total[b, :next_rows] += part

        add(numbers[0], lambda p: main[main_slot[p]], main_halo, main_slot, main_code)
        add(numbers[1], lambda p: held[p], third_halo, third_slot, third_code)
        for b in range(blocks):

            @pl.when(counts[b] > 0)
            def _():
                updated = current[b, pl.ds(next_at, next_rows)] * (
                    total[b, :next_rows] / counts[b].astype(jnp.float32)
                )
                if sweep < ITERS - 1:
                    following[b] = updated
                else:
                    result[b] = updated

            if sweep == ITERS - 1:

                @pl.when(counts[b] == 0)
                def _():
                    at = pl.multiple_of(2 * ITERS * low, 2 * H)
                    result[b] = est[b, pl.ds(at, depth)]

                store = pltpu.make_async_copy(result.at[b], out.at[b], sems.at[b])
                store.start()
                stores.append(store)
    for store in stores:
        store.wait()


def deconvolve(lists, main, parts, main_halo, third_halo, est, matrices, depth, guard):
    blocks, frame, lat = est.shape
    nviews, view_rows = matrices[0].shape[:2]
    sides = len(main_halo)
    thirds = lists[2].shape[0]
    inputs = [main, *parts, *main_halo, *third_halo, est, *matrices]
    return pl.pallas_call(
        functools.partial(deconvolve_kernel, len(parts), sides, guard),
        out_shape=jax.ShapeDtypeStruct((blocks, depth, lat), jnp.float32),
        in_specs=[SMEM] * (1 + len(lists)) + [VMEM] * len(inputs),
        out_specs=pl.BlockSpec(memory_space=pltpu.HBM),
        scratch_shapes=[
            pltpu.VMEM((thirds, depth, lat), jnp.bfloat16),
            pltpu.VMEM((blocks * nviews + 1, view_rows, lat), jnp.float32),
            pltpu.VMEM((blocks, frame - 2 * sides * H, lat), jnp.float32),
            pltpu.VMEM((blocks + 1, frame - 2 * sides * H, lat), jnp.float32),
            pltpu.VMEM((blocks, depth, lat), jnp.float32),
            pltpu.SemaphoreType.DMA((blocks,)),
        ],
        compiler_params=pltpu.CompilerParams(vmem_limit_bytes=24 * 1024 * 1024),
        name="deconvolve",
    )(low_rows()[None], *lists, *inputs)


def local(estimate, views, owners, local_blocks, psf):
    blocks, depth, lat = estimate.shape
    nviews = views.shape[1]
    peers = lax.axis_size("join")
    groups = group_count(peers)
    here = lax.axis_index("join").astype(jnp.int32)
    normed = psf / jnp.sum(psf, axis=1, keepdims=True)
    kernel = normed.astype(jnp.bfloat16)

    packed, *rows = pack(
        views, owners, local_blocks, (here // (peers // groups))[None], peers, groups
    )
    packed, line = lax.optimization_barrier((packed, along_groups(rows)))
    arrived = lax.all_to_all(
        packed.reshape(peers, MAIN, depth, lat), "join", split_axis=0, concat_axis=0, tiled=True
    ).reshape(peers * MAIN, depth, lat)

    parts = among_members(line)
    source = sources_of_parts(groups)
    est_halos = halos([estimate], depth, EST_HALO)
    est = framed(estimate, est_halos, 1)
    matrices = bands(kernel, depth, len(est_halos))
    parts, source, est, matrices = lax.optimization_barrier((parts, source, est, matrices))
    third_halo = halos(parts, depth, VIEW_HALO)
    lists = plan(parts, source, here, blocks, nviews)
    arrived, parts, third_halo, lists, est, matrices = lax.optimization_barrier(
        (arrived, parts, third_halo, lists, est, matrices)
    )

    main_halo = halos([arrived], depth, VIEW_HALO)
    main_slot, main_code, third_slot, third_source, third_code, numbers, any_crowded = lists
    guard = lax.axis_size("view") > 2

    def finish(third_at, thirds, third_halo):
        return deconvolve(
            (main_slot, main_code, third_at, third_code, numbers),
            arrived,
            thirds,
            main_halo,
            third_halo,
            est,
            matrices,
            depth,
            guard,
        )

    def fallback():
        sent = pack_all_thirds(views, owners, peers)
        thirds = lax.all_to_all(sent, "join", split_axis=0, concat_axis=0, tiled=True)
        return finish(third_source, [thirds], halos([thirds], depth, VIEW_HALO))

    return lax.cond(
        any_crowded[0] > 0, fallback, lambda: finish(third_slot, parts, third_halo)
    )


def solution(mesh):
    in_specs = (
        P("join", "view", None),
        P("join", None, "view", None),
        P("join", None),
        P("join", None),
        P(),
    )
    out_specs = P("join", "view", None)
    return jax.shard_map(local, mesh=mesh, in_specs=in_specs, out_specs=out_specs, check_vma=False)
```

```python
import functools

import jax
import jax.numpy as jnp
from jax import lax
from jax.experimental import pallas as pl
from jax.experimental.pallas import tpu as pltpu
from jax.sharding import PartitionSpec as P

H = 16
CAP = 3
MAIN = 2
ITERS = 2
GROUP = 8
TILE = 16
EST_HALO = 2 * ITERS * H
VIEW_HALO = EST_HALO - H

SMEM = pl.BlockSpec(memory_space=pltpu.SMEM)
VMEM = pl.BlockSpec(memory_space=pltpu.VMEM)
ANY = pl.BlockSpec(memory_space=pl.ANY)


def pack_kernel(owners, blocks_of, here, views, main, *refs):
    rows, (table, seen, taken, staged, table_rows, in_sems, out_sems, table_sems) = refs[:-8], refs[-8:]
    blocks, nviews, depth, lat = views.shape
    peers, groups = seen.shape[0], len(rows)
    members = peers // groups
    pairs = [(i, v) for i in range(blocks) for v in range(nviews)]
    loads = [
        pltpu.make_async_copy(views.at[i, v], staged.at[i, v], in_sems.at[i, v]) for i, v in pairs
    ]
    for load in loads:
        load.start()

    @pl.loop(0, peers)
    def _(peer):
        seen[peer] = 0

    for group in range(groups):
        taken[group] = 0

    @pl.loop(0, peers * CAP)
    def _(slot):
        table[slot] = -1

    table[peers * CAP] = 0
    stores = []
    for (i, v), load in zip(pairs, loads):
        owner = owners[i, v]
        order = seen[owner]
        seen[owner] = order + 1
        table[owner * CAP + order] = blocks_of[i, v] * nviews + v
        away = lax.rem(owner // members + groups - here[0], groups)
        in_main = order < MAIN
        in_rows = jnp.logical_and(jnp.logical_not(in_main), taken[away] == 0)
        load.wait()

        @pl.when(in_main)
        def _():
            pltpu.make_async_copy(
                staged.at[i, v], main.at[owner * MAIN + order], out_sems.at[i, v]
            ).start()

        @pl.when(jnp.logical_not(in_main))
        def _():
            table[peers * CAP] = jnp.where(in_rows, table[peers * CAP], 1)
            for k in range(groups):

                @pl.when(jnp.logical_and(in_rows, away == k))
                def _():
                    taken[k] = 1
                    pltpu.make_async_copy(
                        staged.at[i, v], rows[k].at[0, pl.ds(0, depth)], out_sems.at[i, v]
                    ).start()

        stores.append((i, v, jnp.logical_or(in_main, in_rows)))

    lane = lax.broadcasted_iota(jnp.int32, (TILE, lat), 1)
    row = jnp.full((TILE, lat), -1, jnp.int32)
    for slot in range(peers * CAP + 1):
        row = jnp.where(lane == slot, table[slot], row)
    table_rows[...] = row.astype(jnp.float32).astype(table_rows.dtype)
    table_stores = [
        pltpu.make_async_copy(table_rows, rows[k].at[0, pl.ds(depth, TILE)], table_sems.at[k])
        for k in range(groups)
    ]
    for store in table_stores:
        store.start()
    for i, v, stored in stores:

        @pl.when(stored)
        def _():
            pltpu.make_async_copy(staged.at[i, v], main.at[0], out_sems.at[i, v]).wait()

    for store in table_stores:
        store.wait()


def pack(views, owners, blocks_of, here, peers, groups):
    blocks, nviews, depth, lat = views.shape
    assert peers * CAP < lat
    return pl.pallas_call(
        pack_kernel,
        out_shape=(jax.ShapeDtypeStruct((peers * MAIN, depth, lat), views.dtype),)
        + (jax.ShapeDtypeStruct((1, depth + TILE, lat), views.dtype),) * groups,
        in_specs=[SMEM, SMEM, SMEM, ANY],
        out_specs=(ANY,) * (1 + groups),
        scratch_shapes=[
            pltpu.SMEM((peers * CAP + 1,), jnp.int32),
            pltpu.SMEM((peers,), jnp.int32),
            pltpu.SMEM((groups,), jnp.int32),
            pltpu.VMEM(views.shape, views.dtype),
            pltpu.VMEM((TILE, lat), views.dtype),
            pltpu.SemaphoreType.DMA((blocks, nviews)),
            pltpu.SemaphoreType.DMA((blocks, nviews)),
            pltpu.SemaphoreType.DMA((groups,)),
        ],
        name="pack",
    )(owners, blocks_of, here, views)


def all_thirds_kernel(owners, views, out, seen, staged, sems):
    blocks, nviews = views.shape[0], views.shape[1]

    @pl.loop(0, out.shape[0])
    def _(peer):
        seen[peer] = 0

    for i in range(blocks):
        for v in range(nviews):
            owner = owners[i, v]
            order = seen[owner]
            seen[owner] = order + 1

            @pl.when(order >= MAIN)
            def _():
                load = pltpu.make_async_copy(views.at[i, v], staged, sems.at[0])
                load.start()
                load.wait()
                store = pltpu.make_async_copy(staged, out.at[owner], sems.at[1])
                store.start()
                store.wait()


def pack_all_thirds(views, owners, peers):
    depth, lat = views.shape[2:]
    return pl.pallas_call(
        all_thirds_kernel,
        out_shape=jax.ShapeDtypeStruct((peers, depth, lat), views.dtype),
        in_specs=[SMEM, ANY],
        out_specs=ANY,
        scratch_shapes=[
            pltpu.SMEM((peers,), jnp.int32),
            pltpu.VMEM((depth, lat), views.dtype),
            pltpu.SemaphoreType.DMA((2,)),
        ],
        name="all_thirds",
    )(owners, views)


def group_count(peers):
    members = 1
    while peers % (2 * members) == 0 and members * members < peers:
        members *= 2
    return peers // members


def along_groups(rows):
    peers = lax.axis_size("join")
    members = peers // len(rows)
    line = [rows[0]]
    for k in range(1, len(rows)):
        line.append(
            lax.ppermute(rows[k], "join", [(i, (i + k * members) % peers) for i in range(peers)])
        )
    return line


def among_members(line):
    peers = lax.axis_size("join")
    members = peers // len(line)
    line = jnp.concatenate(line, axis=0)
    parts = [line]
    for m in range(1, members):
        parts.append(lax.ppermute(line, "join", [(i, i ^ m) for i in range(peers)]))
    return parts


def sources_of_parts(groups):
    peers = lax.axis_size("join")
    members = peers // groups
    here = lax.axis_index("join")
    at = jnp.arange(peers, dtype=jnp.int32)
    group = lax.rem(here // members + groups - lax.rem(at, groups), groups)
    return group * members + jnp.bitwise_xor(lax.rem(here, members), at // groups)


def ends_kernel(start, *refs):
    blocks, (out, staged, sems) = refs[:-3], refs[-3:]
    width = out.shape[1]
    copies, first = [], 0
    for k, block in enumerate(blocks):
        number = block.shape[0]
        held = staged.at[pl.ds(first, number)]
        rows = block.at[:, pl.ds(pl.multiple_of(start[0], TILE), width)]
        copies.append(
            (
                pltpu.make_async_copy(rows, held, sems.at[0, k]),
                pltpu.make_async_copy(held, out.at[pl.ds(first, number)], sems.at[1, k]),
            )
        )
        first += number
    for load, _ in copies:
        load.start()
    for load, store in copies:
        load.wait()
        store.start()
    for _, store in copies:
        store.wait()


def ends(blocks, start, width):
    if len(blocks) == 1:
        return lax.dynamic_slice_in_dim(blocks[0], start, width, axis=1)
    shape = (sum(block.shape[0] for block in blocks), width, blocks[0].shape[2])
    return pl.pallas_call(
        ends_kernel,
        out_shape=jax.ShapeDtypeStruct(shape, blocks[0].dtype),
        in_specs=[SMEM] + [ANY] * len(blocks),
        out_specs=ANY,
        scratch_shapes=[
            pltpu.VMEM(shape, blocks[0].dtype),
            pltpu.SemaphoreType.DMA((2, len(blocks))),
        ],
        name="ends",
    )(jnp.asarray(start, jnp.int32)[None], *blocks)


def halos(blocks, depth, width):
    count = lax.axis_size("view")
    if count == 1:
        return []
    if count == 2:
        sent = ends(blocks, jnp.where(lax.axis_index("view") == 0, depth - width, 0), width)
        return [lax.ppermute(sent, "view", [(0, 1), (1, 0)])]
    forward = [(i, i + 1) for i in range(count - 1)]
    backward = [(target, source) for source, target in forward]
    low = lax.ppermute(ends(blocks, depth - width, width), "view", forward)
    high = lax.ppermute(ends(blocks, 0, width), "view", backward)
    return [low, high]


def framed(block, sides, dim):
    if not sides:
        return block
    if len(sides) == 2:
        return jnp.concatenate([sides[0], block, sides[1]], axis=dim)
    (side,) = sides
    return jnp.where(
        lax.axis_index("view") == 0,
        jnp.concatenate([block, side], axis=dim),
        jnp.concatenate([side, block], axis=dim),
    )


def low_rows():
    count = lax.axis_size("view")
    if count == 2:
        return jnp.where(lax.axis_index("view") == 0, 0, H).astype(jnp.int32)
    return jnp.int32(0 if count == 1 else H)


def halo_rows(sweep):
    return VIEW_HALO - 2 * H * sweep


def piece_starts(depth, sweep):
    count = lax.axis_size("view")
    width = halo_rows(sweep)
    if count == 1:
        return [jnp.int32(0)]
    if count == 2:
        first = lax.axis_index("view") == 0
        return [jnp.where(first, 0, width), jnp.where(first, depth, 0)]
    return [jnp.int32(width), jnp.int32(0), jnp.int32(width + depth)]


def bands_kernel(shapes, shifts, taps_rows, *refs):
    width = taps_rows.shape[-1]
    nviews = taps_rows.shape[1]

    def band(which, v, shift, rows):
        spread = jnp.broadcast_to(taps_rows[which, v : v + 1, :], (rows, width))
        return pltpu.roll(pltpu.roll(spread, 0, 1, stride=1, stride_axis=0), shift, 1)

    at = 0
    for sweep, pieces in enumerate(shapes):
        forward, mirror = refs[2 * sweep], refs[2 * sweep + 1]
        columns, outs = forward.shape[2], mirror.shape[1]
        lane = lax.broadcasted_iota(jnp.int32, (outs, width), 1)
        for v in range(nviews):
            total = jnp.zeros((outs, width), jnp.float32)
            first = 0
            for piece, rows in enumerate(pieces):
                part = band(0, v, shifts[at + 2 * piece], rows)
                forward[v, first : first + rows] = part[:, :columns].astype(forward.dtype)
                inside = jnp.logical_and(lane >= first, lane < first + rows)
                total = jnp.where(inside, band(1, v, shifts[at + 2 * piece + 1], outs), total)
                first += rows
            mirror[v] = total[:, :first].astype(mirror.dtype)
        at += 2 * len(pieces)


def bands(kernel, depth, sides):
    nviews, taps = kernel.shape
    low = low_rows()
    frame = depth + sides * EST_HALO
    width = -(-(frame + 4 * H) // 128) * 128
    shapes, shifts, outs = [], [], []
    for sweep in range(ITERS):
        pieces = (depth,) + (halo_rows(sweep),) * sides
        first = 0
        for rows, start in zip(pieces, piece_starts(depth, sweep)):
            shifts.append(lax.rem(start + low - H + width, width))
            shifts.append(lax.rem(first - start + low - H + width, width))
            first += rows
        shapes.append(pieces)
        rows_in = frame - 2 * sides * H * sweep
        outs.append(jax.ShapeDtypeStruct((nviews, first, rows_in), jnp.bfloat16))
        outs.append(jax.ShapeDtypeStruct((nviews, rows_in - 2 * sides * H, first), jnp.bfloat16))
    rows = jnp.stack([kernel, kernel[:, ::-1]]).astype(jnp.float32)
    rows = jnp.pad(rows, ((0, 0), (0, 0), (0, width - taps)))
    return pl.pallas_call(
        functools.partial(bands_kernel, shapes),
        out_shape=outs,
        in_specs=[SMEM, VMEM],
        out_specs=[VMEM] * len(outs),
        cost_estimate=pl.CostEstimate(flops=10**11, bytes_accessed=0, transcendentals=0),
        name="bands",
    )(jnp.stack(shifts).astype(jnp.int32), rows)


def plan_kernel(nviews, blocks, here, source, *refs):
    parts, refs = refs[:-11], refs[-11:]
    main_slot, main_code, third_slot, third_source, third_code, numbers, any_crowded = refs[:7]
    tables, rows, scalars, sems = refs[7:]
    per_part, depth, lat = parts[0].shape
    depth -= TILE
    peers = source.shape[0]
    blank = blocks * nviews
    loads = [
        pltpu.make_async_copy(
            part.at[:, pl.ds(depth, TILE)], tables.at[pl.ds(j * per_part, per_part)], sems.at[j]
        )
        for j, part in enumerate(parts)
    ]
    for load in loads:
        load.start()
    for b in range(blocks):
        numbers[2 + b] = 0
    for load in loads:
        load.wait()
    at = lax.broadcasted_iota(jnp.int32, (peers, lat), 0)
    together = jnp.zeros((peers, lat), jnp.float32)
    for t in range(peers):
        row = jnp.broadcast_to(tables[t, :1].astype(jnp.float32), (peers, lat))
        together = jnp.where(at == t, row, together)
    rows[...] = together.astype(jnp.int32)
    copy = pltpu.make_async_copy(rows, scalars, sems.at[len(parts)])
    copy.start()
    copy.wait()

    def enlist(t, carry):
        in_main, in_third, crowded = carry
        for order in range(CAP):
            code = scalars[t, here[0] * CAP + order]
            valid = code >= 0

            @pl.when(valid)
            def _():
                b = code // nviews
                numbers[2 + b] = numbers[2 + b] + 1
                if order < MAIN:
                    main_slot[in_main] = source[t] * MAIN + order
                    main_code[in_main] = code
                else:
                    third_slot[in_third] = t
                    third_source[in_third] = source[t]
                    third_code[in_third] = code

            if order < MAIN:
                in_main = in_main + valid.astype(jnp.int32)
            else:
                in_third = in_third + valid.astype(jnp.int32)
        return in_main, in_third, jnp.maximum(crowded, scalars[t, peers * CAP])

    zero = jnp.int32(0)
    in_main, in_third, crowded = lax.fori_loop(0, peers, enlist, (zero, zero, zero))
    numbers[0] = in_main
    numbers[1] = in_third
    any_crowded[0] = crowded
    for more in range(GROUP - 1):
        main_slot[in_main + more] = main_slot[0]
        main_code[in_main + more] = blank
        third_slot[in_third + more] = third_slot[0]
        third_source[in_third + more] = third_source[0]
        third_code[in_third + more] = blank


def plan(parts, source, here, blocks, nviews):
    peers = source.shape[0]
    lat = parts[0].shape[-1]
    listed = jax.ShapeDtypeStruct((peers * MAIN + GROUP,), jnp.int32)
    thirds = jax.ShapeDtypeStruct((peers + GROUP,), jnp.int32)
    return pl.pallas_call(
        functools.partial(plan_kernel, nviews, blocks),
        out_shape=(listed,) * 2
        + (thirds,) * 3
        + (jax.ShapeDtypeStruct((2 + blocks,), jnp.int32), jax.ShapeDtypeStruct((1,), jnp.int32)),
        in_specs=[SMEM] * 2 + [ANY] * len(parts),
        out_specs=(SMEM,) * 7,
        scratch_shapes=[
            pltpu.VMEM((peers, TILE, lat), parts[0].dtype),
            pltpu.VMEM((peers, lat), jnp.int32),
            pltpu.SMEM((peers, lat), jnp.int32),
            pltpu.SemaphoreType.DMA((len(parts) + 1,)),
        ],
        name="plan",
    )(here[None], source, *parts)


def deconvolve_kernel(nparts, sides, guard, low_ref, *refs):
    main_slot, main_code, third_slot, third_code, numbers = refs[:5]
    main, refs = refs[5], refs[6:]
    parts, refs = refs[:nparts], refs[nparts:]
    main_halo, third_halo, refs = refs[:sides], refs[sides : 2 * sides], refs[2 * sides :]
    est, refs = refs[0], refs[1:]
    bands_of, refs = refs[: 2 * ITERS], refs[2 * ITERS :]
    out, held, recip, following, total, result, sems = refs
    blocks, depth, lat = out.shape
    nviews = bands_of[0].shape[0]
    per_part = parts[0].shape[0]
    low = pl.multiple_of(low_ref[0], H)
    counts = [numbers[2 + b] for b in range(blocks)]
    recip[blocks * nviews] = jnp.zeros(recip.shape[1:], recip.dtype)

    @pl.loop(0, numbers[1])
    def _(p):
        slot = third_slot[p]
        for j, part in enumerate(parts):

            @pl.when(jnp.logical_and(slot >= j * per_part, slot < (j + 1) * per_part))
            def _():
                held[p] = part[slot - j * per_part, :depth]

    stores = []
    for sweep in range(ITERS):
        current = est if sweep == 0 else following
        forward, mirror = bands_of[2 * sweep], bands_of[2 * sweep + 1]
        next_rows, view_rows = mirror.shape[1], mirror.shape[2]
        side_rows = halo_rows(sweep)
        next_at = pl.multiple_of(2 * low, 2 * H)
        halo_at = [pl.multiple_of(2 * sweep * low, 2 * H), 0]
        for b in range(blocks):

            @pl.when(counts[b] > 0)
            def _():
                rounded = current[b].astype(jnp.bfloat16)
                for v in range(nviews):
                    blurred = jnp.dot(forward[v], rounded, preferred_element_type=jnp.float32)
                    inverse = 1.0 / blurred
                    if guard:
                        inverse = jnp.where(blurred > 0, inverse, 0.0)
                    recip[b * nviews + v, :view_rows] = inverse

        total[:, :next_rows] = jnp.zeros((blocks + 1, next_rows, lat), jnp.float32)

        def add(number, held_at, halo, slot_at, code_at):
            @pl.loop(0, (number + (GROUP - 1)) // GROUP)
            def _(group):
                gained = []
                for member in range(GROUP):
                    p = group * GROUP + member
                    code = code_at[p]
                    b = code // nviews
                    pieces = [held_at(p).astype(jnp.float32) * recip[code, :depth]]
                    for side, ref in enumerate(halo):
                        first = depth + side * side_rows
                        rows = ref[slot_at[p], pl.ds(halo_at[side], side_rows)]
                        pieces.append(
                            rows.astype(jnp.float32) * recip[code, first : first + side_rows]
                        )
                    quotient = jnp.concatenate([q.astype(jnp.bfloat16) for q in pieces], axis=0)
                    part = jnp.dot(
                        mirror[code - b * nviews], quotient, preferred_element_type=jnp.float32
                    )
                    gained.append((b, part))
                for b, part in gained:
                    total[b, :next_rows] += part

        add(numbers[0], lambda p: main[main_slot[p]], main_halo, main_slot, main_code)
        add(numbers[1], lambda p: held[p], third_halo, third_slot, third_code)
        for b in range(blocks):

            @pl.when(counts[b] > 0)
            def _():
                updated = current[b, pl.ds(next_at, next_rows)] * (
                    total[b, :next_rows] / counts[b].astype(jnp.float32)
                )
                if sweep < ITERS - 1:
                    following[b] = updated
                else:
                    result[b] = updated

            if sweep == ITERS - 1:

                @pl.when(counts[b] == 0)
                def _():
                    at = pl.multiple_of(2 * ITERS * low, 2 * H)
                    result[b] = est[b, pl.ds(at, depth)]

                store = pltpu.make_async_copy(result.at[b], out.at[b], sems.at[b])
                store.start()
                stores.append(store)
    for store in stores:
        store.wait()


def deconvolve(lists, main, parts, main_halo, third_halo, est, matrices, depth, guard):
    blocks, frame, lat = est.shape
    nviews, view_rows = matrices[0].shape[:2]
    sides = len(main_halo)
    thirds = lists[2].shape[0]
    inputs = [main, *parts, *main_halo, *third_halo, est, *matrices]
    return pl.pallas_call(
        functools.partial(deconvolve_kernel, len(parts), sides, guard),
        out_shape=jax.ShapeDtypeStruct((blocks, depth, lat), jnp.float32),
        in_specs=[SMEM] * (1 + len(lists)) + [VMEM] * len(inputs),
        out_specs=pl.BlockSpec(memory_space=pltpu.HBM),
        scratch_shapes=[
            pltpu.VMEM((thirds, depth, lat), jnp.bfloat16),
            pltpu.VMEM((blocks * nviews + 1, view_rows, lat), jnp.float32),
            pltpu.VMEM((blocks, frame - 2 * sides * H, lat), jnp.float32),
            pltpu.VMEM((blocks + 1, frame - 2 * sides * H, lat), jnp.float32),
            pltpu.VMEM((blocks, depth, lat), jnp.float32),
            pltpu.SemaphoreType.DMA((blocks,)),
        ],
        compiler_params=pltpu.CompilerParams(vmem_limit_bytes=24 * 1024 * 1024),
        name="deconvolve",
    )(low_rows()[None], *lists, *inputs)


def local(estimate, views, owners, local_blocks, psf):
    blocks, depth, lat = estimate.shape
    nviews = views.shape[1]
    peers = lax.axis_size("join")
    groups = group_count(peers)
    here = lax.axis_index("join").astype(jnp.int32)
    normed = psf / jnp.sum(psf, axis=1, keepdims=True)
    kernel = normed.astype(jnp.bfloat16)

    packed, *rows = pack(
        views, owners, local_blocks, (here // (peers // groups))[None], peers, groups
    )
    line = along_groups(rows)
    arrived = lax.all_to_all(
        packed.reshape(peers, MAIN, depth, lat), "join", split_axis=0, concat_axis=0, tiled=True
    ).reshape(peers * MAIN, depth, lat)

    parts = among_members(line)
    source = sources_of_parts(groups)
    kernel, estimate, line = lax.optimization_barrier((kernel, estimate, line))
    est_halos = halos([estimate], depth, EST_HALO)
    est = framed(estimate, est_halos, 1)
    matrices = bands(kernel, depth, len(est_halos))
    parts, source, est, matrices = lax.optimization_barrier((parts, source, est, matrices))
    third_halo = halos(parts, depth, VIEW_HALO)
    lists = plan(parts, source, here, blocks, nviews)
    arrived, parts, third_halo, lists, est, matrices = lax.optimization_barrier(
        (arrived, parts, third_halo, lists, est, matrices)
    )

    main_halo = halos([arrived], depth, VIEW_HALO)
    main_slot, main_code, third_slot, third_source, third_code, numbers, any_crowded = lists
    guard = lax.axis_size("view") > 2

    def finish(third_at, thirds, third_halo):
        return deconvolve(
            (main_slot, main_code, third_at, third_code, numbers),
            arrived,
            thirds,
            main_halo,
            third_halo,
            est,
            matrices,
            depth,
            guard,
        )

    def fallback():
        sent = pack_all_thirds(views, owners, peers)
        thirds = lax.all_to_all(sent, "join", split_axis=0, concat_axis=0, tiled=True)
        return finish(third_source, [thirds], halos([thirds], depth, VIEW_HALO))

    return lax.cond(
        any_crowded[0] > 0, fallback, lambda: finish(third_slot, parts, third_halo)
    )


def solution(mesh):
    in_specs = (
        P("join", "view", None),
        P("join", None, "view", None),
        P("join", None),
        P("join", None),
        P(),
    )
    out_specs = P("join", "view", None)
    return jax.shard_map(local, mesh=mesh, in_specs=in_specs, out_specs=out_specs, check_vma=False)
```

```python
import functools

import jax
import jax.numpy as jnp
from jax import lax
from jax.experimental import pallas as pl
from jax.experimental.pallas import tpu as pltpu
from jax.sharding import PartitionSpec as P

H = 16
CAP = 3
MAIN = 2
ITERS = 2
GROUP = 16
TILE = 16
EST_HALO = 2 * ITERS * H
VIEW_HALO = EST_HALO - H

SMEM = pl.BlockSpec(memory_space=pltpu.SMEM)
VMEM = pl.BlockSpec(memory_space=pltpu.VMEM)
ANY = pl.BlockSpec(memory_space=pl.ANY)
HBM = pl.BlockSpec(memory_space=pltpu.HBM)


def pack_kernel(owners, blocks_of, here, views, main, *refs):
    rows, (table, seen, taken, staged, table_rows, in_sems, out_sems, table_sems) = refs[:-8], refs[-8:]
    blocks, nviews, depth, lat = views.shape
    peers, groups = seen.shape[0], len(rows)
    members = peers // groups
    pairs = [(i, v) for i in range(blocks) for v in range(nviews)]
    loads = [
        pltpu.make_async_copy(views.at[i, v], staged.at[i, v], in_sems.at[i, v]) for i, v in pairs
    ]
    for load in loads:
        load.start()

    @pl.loop(0, peers)
    def _(peer):
        seen[peer] = 0

    for group in range(groups):
        taken[group] = 0

    @pl.loop(0, peers * CAP)
    def _(slot):
        table[slot] = -1

    table[peers * CAP] = 0
    stores = []
    for (i, v), load in zip(pairs, loads):
        owner = owners[i, v]
        order = seen[owner]
        seen[owner] = order + 1
        table[owner * CAP + order] = blocks_of[i, v] * nviews + v
        away = lax.rem(owner // members + groups - here[0], groups)
        in_main = order < MAIN
        in_rows = jnp.logical_and(jnp.logical_not(in_main), taken[away] == 0)
        load.wait()

        @pl.when(in_main)
        def _():
            pltpu.make_async_copy(
                staged.at[i, v], main.at[owner * MAIN + order], out_sems.at[i, v]
            ).start()

        @pl.when(jnp.logical_not(in_main))
        def _():
            table[peers * CAP] = jnp.where(in_rows, table[peers * CAP], 1)
            for k in range(groups):

                @pl.when(jnp.logical_and(in_rows, away == k))
                def _():
                    taken[k] = 1
                    pltpu.make_async_copy(
                        staged.at[i, v], rows[k].at[0, pl.ds(0, depth)], out_sems.at[i, v]
                    ).start()

        stores.append((i, v, jnp.logical_or(in_main, in_rows)))

    lane = lax.broadcasted_iota(jnp.int32, (TILE, lat), 1)
    row = jnp.full((TILE, lat), -1, jnp.int32)
    for slot in range(peers * CAP + 1):
        row = jnp.where(lane == slot, table[slot], row)
    table_rows[...] = row.astype(jnp.float32).astype(table_rows.dtype)
    table_stores = [
        pltpu.make_async_copy(table_rows, rows[k].at[0, pl.ds(depth, TILE)], table_sems.at[k])
        for k in range(groups)
    ]
    for store in table_stores:
        store.start()
    for i, v, stored in stores:

        @pl.when(stored)
        def _():
            pltpu.make_async_copy(staged.at[i, v], main.at[0], out_sems.at[i, v]).wait()

    for store in table_stores:
        store.wait()


def pack(views, owners, blocks_of, here, peers, groups):
    blocks, nviews, depth, lat = views.shape
    assert peers * CAP < lat
    return pl.pallas_call(
        pack_kernel,
        out_shape=(jax.ShapeDtypeStruct((peers * MAIN, depth, lat), views.dtype),)
        + (jax.ShapeDtypeStruct((1, depth + TILE, lat), views.dtype),) * groups,
        in_specs=[SMEM, SMEM, SMEM, ANY],
        out_specs=(ANY,) * (1 + groups),
        scratch_shapes=[
            pltpu.SMEM((peers * CAP + 1,), jnp.int32),
            pltpu.SMEM((peers,), jnp.int32),
            pltpu.SMEM((groups,), jnp.int32),
            pltpu.VMEM(views.shape, views.dtype),
            pltpu.VMEM((TILE, lat), views.dtype),
            pltpu.SemaphoreType.DMA((blocks, nviews)),
            pltpu.SemaphoreType.DMA((blocks, nviews)),
            pltpu.SemaphoreType.DMA((groups,)),
        ],
        name="pack",
    )(owners, blocks_of, here, views)


def all_thirds_kernel(owners, views, out, seen, staged, sems):
    blocks, nviews = views.shape[0], views.shape[1]

    @pl.loop(0, out.shape[0])
    def _(peer):
        seen[peer] = 0

    for i in range(blocks):
        for v in range(nviews):
            owner = owners[i, v]
            order = seen[owner]
            seen[owner] = order + 1

            @pl.when(order >= MAIN)
            def _():
                load = pltpu.make_async_copy(views.at[i, v], staged, sems.at[0])
                load.start()
                load.wait()
                store = pltpu.make_async_copy(staged, out.at[owner], sems.at[1])
                store.start()
                store.wait()


def pack_all_thirds(views, owners, peers):
    depth, lat = views.shape[2:]
    return pl.pallas_call(
        all_thirds_kernel,
        out_shape=jax.ShapeDtypeStruct((peers, depth, lat), views.dtype),
        in_specs=[SMEM, ANY],
        out_specs=ANY,
        scratch_shapes=[
            pltpu.SMEM((peers,), jnp.int32),
            pltpu.VMEM((depth, lat), views.dtype),
            pltpu.SemaphoreType.DMA((2,)),
        ],
        name="all_thirds",
    )(owners, views)


def group_count(peers):
    members = 1
    while peers % (2 * members) == 0 and members * members < peers:
        members *= 2
    return peers // members


def along_groups(rows):
    peers = lax.axis_size("join")
    members = peers // len(rows)
    line = [rows[0]]
    for k in range(1, len(rows)):
        line.append(
            lax.ppermute(rows[k], "join", [(i, (i + k * members) % peers) for i in range(peers)])
        )
    return line


def among_members(line):
    peers = lax.axis_size("join")
    members = peers // len(line)
    line = jnp.concatenate(line, axis=0)
    parts = [line]
    for m in range(1, members):
        parts.append(lax.ppermute(line, "join", [(i, i ^ m) for i in range(peers)]))
    return parts


def sources_of_parts(groups):
    peers = lax.axis_size("join")
    members = peers // groups
    here = lax.axis_index("join")
    at = jnp.arange(peers, dtype=jnp.int32)
    group = lax.rem(here // members + groups - lax.rem(at, groups), groups)
    return group * members + jnp.bitwise_xor(lax.rem(here, members), at // groups)


def ends_kernel(start, *refs):
    blocks, (out, staged, sems) = refs[:-3], refs[-3:]
    width = out.shape[1]
    copies, first = [], 0
    for k, block in enumerate(blocks):
        number = block.shape[0]
        held = staged.at[pl.ds(first, number)]
        rows = block.at[:, pl.ds(pl.multiple_of(start[0], TILE), width)]
        copies.append(
            (
                pltpu.make_async_copy(rows, held, sems.at[0, k]),
                pltpu.make_async_copy(held, out.at[pl.ds(first, number)], sems.at[1, k]),
            )
        )
        first += number
    for load, _ in copies:
        load.start()
    for load, store in copies:
        load.wait()
        store.start()
    for _, store in copies:
        store.wait()


def ends(blocks, start, width):
    if len(blocks) == 1:
        return lax.dynamic_slice_in_dim(blocks[0], start, width, axis=1)
    shape = (sum(block.shape[0] for block in blocks), width, blocks[0].shape[2])
    return pl.pallas_call(
        ends_kernel,
        out_shape=jax.ShapeDtypeStruct(shape, blocks[0].dtype),
        in_specs=[SMEM] + [ANY] * len(blocks),
        out_specs=ANY,
        scratch_shapes=[
            pltpu.VMEM(shape, blocks[0].dtype),
            pltpu.SemaphoreType.DMA((2, len(blocks))),
        ],
        name="ends",
    )(jnp.asarray(start, jnp.int32)[None], *blocks)


def halos(blocks, depth, width):
    count = lax.axis_size("view")
    if count == 1:
        return []
    if count == 2:
        sent = ends(blocks, jnp.where(lax.axis_index("view") == 0, depth - width, 0), width)
        return [lax.ppermute(sent, "view", [(0, 1), (1, 0)])]
    forward = [(i, i + 1) for i in range(count - 1)]
    backward = [(target, source) for source, target in forward]
    low = lax.ppermute(ends(blocks, depth - width, width), "view", forward)
    high = lax.ppermute(ends(blocks, 0, width), "view", backward)
    return [low, high]


def framed(block, sides, dim):
    if not sides:
        return block
    if len(sides) == 2:
        return jnp.concatenate([sides[0], block, sides[1]], axis=dim)
    (side,) = sides
    return jnp.where(
        lax.axis_index("view") == 0,
        jnp.concatenate([block, side], axis=dim),
        jnp.concatenate([side, block], axis=dim),
    )


def low_rows():
    count = lax.axis_size("view")
    if count == 2:
        return jnp.where(lax.axis_index("view") == 0, 0, H).astype(jnp.int32)
    return jnp.int32(0 if count == 1 else H)


def halo_rows(sweep):
    return VIEW_HALO - 2 * H * sweep


def piece_starts(depth, sweep):
    count = lax.axis_size("view")
    width = halo_rows(sweep)
    if count == 1:
        return [jnp.int32(0)]
    if count == 2:
        first = lax.axis_index("view") == 0
        return [jnp.where(first, 0, width), jnp.where(first, depth, 0)]
    return [jnp.int32(width), jnp.int32(0), jnp.int32(width + depth)]


def bands_kernel(shapes, shifts, taps_rows, *refs):
    width = taps_rows.shape[-1]
    nviews = taps_rows.shape[1]

    def band(which, v, shift, rows):
        spread = jnp.broadcast_to(taps_rows[which, v : v + 1, :], (rows, width))
        return pltpu.roll(pltpu.roll(spread, 0, 1, stride=1, stride_axis=0), shift, 1)

    at = 0
    for sweep, pieces in enumerate(shapes):
        forward, mirror = refs[2 * sweep], refs[2 * sweep + 1]
        columns, outs = forward.shape[2], mirror.shape[1]
        lane = lax.broadcasted_iota(jnp.int32, (outs, width), 1)
        for v in range(nviews):
            total = jnp.zeros((outs, width), jnp.float32)
            first = 0
            for piece, rows in enumerate(pieces):
                part = band(0, v, shifts[at + 2 * piece], rows)
                forward[v, first : first + rows] = part[:, :columns].astype(forward.dtype)
                inside = jnp.logical_and(lane >= first, lane < first + rows)
                total = jnp.where(inside, band(1, v, shifts[at + 2 * piece + 1], outs), total)
                first += rows
            mirror[v] = total[:, :first].astype(mirror.dtype)
        at += 2 * len(pieces)


def bands(kernel, depth, sides):
    nviews, taps = kernel.shape
    low = low_rows()
    frame = depth + sides * EST_HALO
    width = -(-(frame + 4 * H) // 128) * 128
    shapes, shifts, outs = [], [], []
    for sweep in range(ITERS):
        pieces = (depth,) + (halo_rows(sweep),) * sides
        first = 0
        for rows, start in zip(pieces, piece_starts(depth, sweep)):
            shifts.append(lax.rem(start + low - H + width, width))
            shifts.append(lax.rem(first - start + low - H + width, width))
            first += rows
        shapes.append(pieces)
        rows_in = frame - 2 * sides * H * sweep
        outs.append(jax.ShapeDtypeStruct((nviews, first, rows_in), jnp.bfloat16))
        outs.append(jax.ShapeDtypeStruct((nviews, rows_in - 2 * sides * H, first), jnp.bfloat16))
    rows = jnp.stack([kernel, kernel[:, ::-1]]).astype(jnp.float32)
    rows = jnp.pad(rows, ((0, 0), (0, 0), (0, width - taps)))
    return pl.pallas_call(
        functools.partial(bands_kernel, shapes),
        out_shape=outs,
        in_specs=[SMEM, VMEM],
        out_specs=[VMEM] * len(outs),
        cost_estimate=pl.CostEstimate(flops=10**11, bytes_accessed=0, transcendentals=0),
        name="bands",
    )(jnp.stack(shifts).astype(jnp.int32), rows)


def list_starts(peers):
    main, third = peers * MAIN + GROUP, peers + GROUP
    return 0, main, 2 * main, 2 * main + third, 2 * main + 2 * third, 2 * main + 3 * third


def plan_kernel(nviews, blocks, place, source, *refs):
    parts, (lists, any_crowded, tables, rows, scalars, sems) = refs[:-6], refs[-6:]
    per_part, depth, lat = parts[0].shape
    depth -= TILE
    peers = source.shape[0]
    blank = blocks * nviews
    main_slot, main_code, third_slot, third_source, third_code, numbers = list_starts(peers)
    loads = [
        pltpu.make_async_copy(
            part.at[:, pl.ds(depth, TILE)], tables.at[pl.ds(j * per_part, per_part)], sems.at[j]
        )
        for j, part in enumerate(parts)
    ]
    for load in loads:
        load.start()
    lists[numbers + 2] = place[1]
    for b in range(blocks):
        lists[numbers + 3 + b] = 0
    for load in loads:
        load.wait()
    at = lax.broadcasted_iota(jnp.int32, (peers, lat), 0)
    together = jnp.zeros((peers, lat), jnp.float32)
    for t in range(peers):
        row = jnp.broadcast_to(tables[t, :1].astype(jnp.float32), (peers, lat))
        together = jnp.where(at == t, row, together)
    rows[...] = together.astype(jnp.int32)
    copy = pltpu.make_async_copy(rows, scalars, sems.at[len(parts)])
    copy.start()
    copy.wait()

    def enlist(t, carry):
        in_main, in_third, crowded = carry
        for order in range(CAP):
            code = scalars[t, place[0] * CAP + order]
            valid = code >= 0

            @pl.when(valid)
            def _():
                at = numbers + 3 + code // nviews
                lists[at] = lists[at] + 1
                if order < MAIN:
                    lists[main_slot + in_main] = source[t] * MAIN + order
                    lists[main_code + in_main] = code
                else:
                    lists[third_slot + in_third] = t
                    lists[third_source + in_third] = source[t]
                    lists[third_code + in_third] = code

            if order < MAIN:
                in_main = in_main + valid.astype(jnp.int32)
            else:
                in_third = in_third + valid.astype(jnp.int32)
        return in_main, in_third, jnp.maximum(crowded, scalars[t, peers * CAP])

    zero = jnp.int32(0)
    in_main, in_third, crowded = lax.fori_loop(0, peers, enlist, (zero, zero, zero))
    lists[numbers] = in_main
    lists[numbers + 1] = in_third
    any_crowded[0] = crowded
    for more in range(GROUP - 1):
        lists[main_slot + in_main + more] = lists[main_slot]
        lists[main_code + in_main + more] = blank
        lists[third_code + in_third + more] = blank


def plan(parts, source, here, blocks, nviews):
    peers = source.shape[0]
    lat = parts[0].shape[-1]
    length = list_starts(peers)[-1] + 3 + blocks
    return pl.pallas_call(
        functools.partial(plan_kernel, nviews, blocks),
        out_shape=(
            jax.ShapeDtypeStruct((length,), jnp.int32),
            jax.ShapeDtypeStruct((1,), jnp.int32),
        ),
        in_specs=[SMEM] * 2 + [ANY] * len(parts),
        out_specs=(SMEM,) * 2,
        scratch_shapes=[
            pltpu.VMEM((peers, TILE, lat), parts[0].dtype),
            pltpu.VMEM((peers, lat), jnp.int32),
            pltpu.SMEM((peers, lat), jnp.int32),
            pltpu.SemaphoreType.DMA((len(parts) + 1,)),
        ],
        name="plan",
    )(jnp.stack([here, low_rows()]), source, *parts)


def deconvolve_kernel(starts, nparts, sides, guard, lists, main, est, *refs):
    main_slot, main_code, third_slot, third_code, numbers = starts
    parts, third_halo, refs = refs[:nparts], refs[nparts : nparts + sides], refs[nparts + sides :]
    number = 2 * ITERS + sides
    sources, out, refs = refs[:number], refs[number], refs[number + 1 :]
    copied, refs = refs[:number], refs[number:]
    bands_of, main_halo = copied[: 2 * ITERS], copied[2 * ITERS :]
    held, recip, following, total, result, own_sems, held_sems, out_sems = refs
    blocks, depth, lat = out.shape
    nviews = bands_of[0].shape[0]
    per_part = parts[0].shape[0]
    mains, thirds = lists[numbers], lists[numbers + 1]
    low = pl.multiple_of(lists[numbers + 2], H)
    counts = [lists[numbers + 3 + b] for b in range(blocks)]
    own = [
        pltpu.make_async_copy(source, to, own_sems.at[k])
        for k, (source, to) in enumerate(zip(sources, copied))
    ]
    for copy in own:
        copy.start()

    def copies(p, part, at, slot):
        yield pltpu.make_async_copy(
            part.at[at, pl.ds(0, depth)], held.at[p, pl.ds(0, depth)], held_sems.at[p, 0]
        )
        for side, ref in enumerate(third_halo):
            rows = pl.ds(depth + side * VIEW_HALO, VIEW_HALO)
            yield pltpu.make_async_copy(ref.at[slot], held.at[p, rows], held_sems.at[p, 1 + side])

    @pl.loop(0, thirds)
    def _(p):
        slot = lists[third_slot + p]
        for j, part in enumerate(parts):

            @pl.when(jnp.logical_and(slot >= j * per_part, slot < (j + 1) * per_part))
            def _():
                for copy in copies(p, part, slot - j * per_part, slot):
                    copy.start()

    @pl.loop(thirds, (thirds + (GROUP - 1)) // GROUP * GROUP)
    def _(p):
        held[p] = jnp.zeros(held.shape[1:], held.dtype)

    recip[blocks * nviews] = jnp.zeros(recip.shape[1:], recip.dtype)
    stores = []
    for sweep in range(ITERS):
        current = est if sweep == 0 else following
        forward, mirror = bands_of[2 * sweep], bands_of[2 * sweep + 1]
        next_rows, view_rows = mirror.shape[1], mirror.shape[2]
        side_rows = halo_rows(sweep)
        next_at = pl.multiple_of(2 * low, 2 * H)
        halo_at = [pl.multiple_of(2 * sweep * low, 2 * H), 0]
        own[2 * sweep].wait()
        for b in range(blocks):

            @pl.when(counts[b] > 0)
            def _():
                rounded = current[b, : forward.shape[2]].astype(jnp.bfloat16)
                for v in range(nviews):
                    blurred = jnp.dot(forward[v], rounded, preferred_element_type=jnp.float32)
                    inverse = 1.0 / blurred
                    if guard:
                        inverse = jnp.where(blurred > 0, inverse, 0.0)
                    recip[b * nviews + v, :view_rows] = inverse

        total[:, :next_rows] = jnp.zeros((blocks + 1, next_rows, lat), jnp.float32)

        def main_rows(p):
            slot = lists[main_slot + p]
            rows = [main[slot]]
            for side, ref in enumerate(main_halo):
                rows.append(ref[slot, pl.ds(halo_at[side], side_rows)])
            return rows

        def third_rows(p):
            rows = [held[p, :depth]]
            for side in range(sides):
                at = depth + side * VIEW_HALO + halo_at[side]
                rows.append(held[p, pl.ds(pl.multiple_of(at, H), side_rows)])
            return rows

        def add(number, rows_of, code_at):
            @pl.loop(0, (number + (GROUP - 1)) // GROUP)
            def _(group):
                gained = []
                for member in range(GROUP):
                    p = group * GROUP + member
                    code = lists[code_at + p]
                    b = code // nviews
                    pieces, first = [], 0
                    for rows in rows_of(p):
                        last = first + rows.shape[0]
                        quotient = rows.astype(jnp.float32) * recip[code, first:last]
                        pieces.append(quotient.astype(jnp.bfloat16))
                        first = last
                    part = jnp.dot(
                        mirror[code - b * nviews],
                        jnp.concatenate(pieces, axis=0),
                        preferred_element_type=jnp.float32,
                    )
                    gained.append((b, part))
                for b, part in gained:
                    total[b, :next_rows] += part

        own[2 * sweep + 1].wait()
        if sweep == 0:
            for copy in own[2 * ITERS :]:
                copy.wait()
        add(mains, main_rows, main_code)
        if sweep == 0:

            @pl.loop(0, thirds)
            def _(p):
                for copy in copies(p, parts[0], 0, 0):
                    copy.wait()

        add(thirds, third_rows, third_code)
        for b in range(blocks):

            @pl.when(counts[b] > 0)
            def _():
                updated = current[b, pl.ds(next_at, next_rows)] * (
                    total[b, :next_rows] / counts[b].astype(jnp.float32)
                )
                if sweep < ITERS - 1:
                    following[b, :next_rows] = updated
                else:
                    result[b] = updated

            if sweep == ITERS - 1:

                @pl.when(counts[b] == 0)
                def _():
                    at = pl.multiple_of(2 * ITERS * low, 2 * H)
                    result[b] = est[b, pl.ds(at, depth)]

                store = pltpu.make_async_copy(result.at[b], out.at[b], out_sems.at[b])
                store.start()
                stores.append(store)
    for store in stores:
        store.wait()


def deconvolve(lists, starts, main, parts, main_halo, third_halo, est, matrices, depth, guard):
    blocks, frame, lat = est.shape
    nviews, view_rows = matrices[0].shape[:2]
    sides = len(main_halo)
    thirds = parts[0].shape[0] * len(parts) + GROUP
    following = (frame - 2 * sides * H, lat)
    copied = [*matrices, *main_halo]
    in_place = [*parts, *third_halo, *copied]
    return pl.pallas_call(
        functools.partial(deconvolve_kernel, starts, len(parts), sides, guard),
        out_shape=pltpu.HBM((blocks, depth, lat), jnp.float32),
        in_specs=[SMEM] + [VMEM] * 2 + [ANY] * len(in_place),
        out_specs=HBM,
        scratch_shapes=[pltpu.VMEM(array.shape, array.dtype) for array in copied]
        + [
            pltpu.VMEM((thirds, view_rows, lat), jnp.bfloat16),
            pltpu.VMEM((blocks * nviews + 1, view_rows, lat), jnp.float32),
            pltpu.VMEM((blocks, *following), jnp.float32),
            pltpu.VMEM((blocks + 1, *following), jnp.float32),
            pltpu.VMEM((blocks, depth, lat), jnp.float32),
            pltpu.SemaphoreType.DMA((len(copied),)),
            pltpu.SemaphoreType.DMA((thirds, 1 + sides)),
            pltpu.SemaphoreType.DMA((blocks,)),
        ],
        compiler_params=pltpu.CompilerParams(vmem_limit_bytes=24 * 1024 * 1024),
        name="deconvolve",
    )(lists, main, est, *in_place)


def local(estimate, views, owners, local_blocks, psf):
    blocks, depth, lat = estimate.shape
    nviews = views.shape[1]
    peers = lax.axis_size("join")
    groups = group_count(peers)
    here = lax.axis_index("join").astype(jnp.int32)
    normed = psf / jnp.sum(psf, axis=1, keepdims=True)
    kernel = normed.astype(jnp.bfloat16)

    packed, *rows = pack(
        views, owners, local_blocks, (here // (peers // groups))[None], peers, groups
    )
    line = along_groups(rows)
    arrived = lax.all_to_all(
        packed.reshape(peers, MAIN, depth, lat), "join", split_axis=0, concat_axis=0, tiled=True
    ).reshape(peers * MAIN, depth, lat)

    parts = among_members(line)
    source = sources_of_parts(groups)
    kernel, estimate, line = lax.optimization_barrier((kernel, estimate, line))
    est_halos = halos([estimate], depth, EST_HALO)
    est = framed(estimate, est_halos, 1)
    matrices = bands(kernel, depth, len(est_halos))
    parts, source, est, matrices = lax.optimization_barrier((parts, source, est, matrices))
    third_halo = halos(parts, depth, VIEW_HALO)
    planned = plan(parts, source, here, blocks, nviews)
    arrived, parts, third_halo, planned, est, matrices = lax.optimization_barrier(
        (arrived, parts, third_halo, planned, est, matrices)
    )
    lists, any_crowded = planned
    main_slot, main_code, third_slot, third_source, third_code, numbers = list_starts(peers)

    main_halo = halos([arrived], depth, VIEW_HALO)
    guard = lax.axis_size("view") > 2

    def finish(third_at, thirds, third_halo):
        return deconvolve(
            lists,
            (main_slot, main_code, third_at, third_code, numbers),
            arrived,
            thirds,
            main_halo,
            third_halo,
            est,
            matrices,
            depth,
            guard,
        )

    def fallback():
        sent = pack_all_thirds(views, owners, peers)
        thirds = lax.all_to_all(sent, "join", split_axis=0, concat_axis=0, tiled=True)
        return finish(third_source, [thirds], halos([thirds], depth, VIEW_HALO))

    return lax.cond(
        any_crowded[0] > 0, fallback, lambda: finish(third_slot, parts, third_halo)
    )


def solution(mesh):
    in_specs = (
        P("join", "view", None),
        P("join", None, "view", None),
        P("join", None),
        P("join", None),
        P(),
    )
    out_specs = P("join", "view", None)
    return jax.shard_map(local, mesh=mesh, in_specs=in_specs, out_specs=out_specs, check_vma=False)
```

```python
import functools

import jax
import jax.numpy as jnp
from jax import lax
from jax.experimental import pallas as pl
from jax.experimental.pallas import tpu as pltpu
from jax.sharding import PartitionSpec as P

H = 16
CAP = 3
MAIN = 2
ITERS = 2
GROUP = 16
TILE = 16
EST_HALO = 2 * ITERS * H
VIEW_HALO = EST_HALO - H

SMEM = pl.BlockSpec(memory_space=pltpu.SMEM)
VMEM = pl.BlockSpec(memory_space=pltpu.VMEM)
ANY = pl.BlockSpec(memory_space=pl.ANY)
HBM = pl.BlockSpec(memory_space=pltpu.HBM)


def pack_kernel(owners, blocks_of, here, views, main, *refs):
    rows, (table, seen, taken, staged, table_rows, in_sems, out_sems, table_sems) = refs[:-8], refs[-8:]
    blocks, nviews, depth, lat = views.shape
    peers, groups = seen.shape[0], len(rows)
    members = peers // groups
    pairs = [(i, v) for i in range(blocks) for v in range(nviews)]
    loads = [
        pltpu.make_async_copy(views.at[i, v], staged.at[i, v], in_sems.at[i, v]) for i, v in pairs
    ]
    for load in loads:
        load.start()

    @pl.loop(0, peers)
    def _(peer):
        seen[peer] = 0

    for group in range(groups):
        taken[group] = 0

    @pl.loop(0, peers * CAP)
    def _(slot):
        table[slot] = -1

    table[peers * CAP] = 0
    stores = []
    for (i, v), load in zip(pairs, loads):
        owner = owners[i, v]
        order = seen[owner]
        seen[owner] = order + 1
        table[owner * CAP + order] = blocks_of[i, v] * nviews + v
        away = lax.rem(owner // members + groups - here[0], groups)
        in_main = order < MAIN
        in_rows = jnp.logical_and(jnp.logical_not(in_main), taken[away] == 0)
        load.wait()

        @pl.when(in_main)
        def _():
            pltpu.make_async_copy(
                staged.at[i, v], main.at[owner * MAIN + order], out_sems.at[i, v]
            ).start()

        @pl.when(jnp.logical_not(in_main))
        def _():
            table[peers * CAP] = jnp.where(in_rows, table[peers * CAP], 1)
            for k in range(groups):

                @pl.when(jnp.logical_and(in_rows, away == k))
                def _():
                    taken[k] = 1
                    pltpu.make_async_copy(
                        staged.at[i, v], rows[k].at[0, pl.ds(0, depth)], out_sems.at[i, v]
                    ).start()

        stores.append((i, v, jnp.logical_or(in_main, in_rows)))

    lane = lax.broadcasted_iota(jnp.int32, (TILE, lat), 1)
    row = jnp.full((TILE, lat), -1, jnp.int32)
    for slot in range(peers * CAP + 1):
        row = jnp.where(lane == slot, table[slot], row)
    table_rows[...] = row.astype(jnp.float32).astype(table_rows.dtype)
    table_stores = [
        pltpu.make_async_copy(table_rows, rows[k].at[0, pl.ds(depth, TILE)], table_sems.at[k])
        for k in range(groups)
    ]
    for store in table_stores:
        store.start()
    for i, v, stored in stores:

        @pl.when(stored)
        def _():
            pltpu.make_async_copy(staged.at[i, v], main.at[0], out_sems.at[i, v]).wait()

    for store in table_stores:
        store.wait()


def pack(views, owners, blocks_of, here, peers, groups):
    blocks, nviews, depth, lat = views.shape
    assert peers * CAP < lat
    return pl.pallas_call(
        pack_kernel,
        out_shape=(jax.ShapeDtypeStruct((peers * MAIN, depth, lat), views.dtype),)
        + (jax.ShapeDtypeStruct((1, depth + TILE, lat), views.dtype),) * groups,
        in_specs=[SMEM, SMEM, SMEM, ANY],
        out_specs=(ANY,) * (1 + groups),
        scratch_shapes=[
            pltpu.SMEM((peers * CAP + 1,), jnp.int32),
            pltpu.SMEM((peers,), jnp.int32),
            pltpu.SMEM((groups,), jnp.int32),
            pltpu.VMEM(views.shape, views.dtype),
            pltpu.VMEM((TILE, lat), views.dtype),
            pltpu.SemaphoreType.DMA((blocks, nviews)),
            pltpu.SemaphoreType.DMA((blocks, nviews)),
            pltpu.SemaphoreType.DMA((groups,)),
        ],
        name="pack",
    )(owners, blocks_of, here, views)


def all_thirds_kernel(owners, views, out, seen, staged, sems):
    blocks, nviews = views.shape[0], views.shape[1]

    @pl.loop(0, out.shape[0])
    def _(peer):
        seen[peer] = 0

    for i in range(blocks):
        for v in range(nviews):
            owner = owners[i, v]
            order = seen[owner]
            seen[owner] = order + 1

            @pl.when(order >= MAIN)
            def _():
                load = pltpu.make_async_copy(views.at[i, v], staged, sems.at[0])
                load.start()
                load.wait()
                store = pltpu.make_async_copy(staged, out.at[owner], sems.at[1])
                store.start()
                store.wait()


def pack_all_thirds(views, owners, peers):
    depth, lat = views.shape[2:]
    return pl.pallas_call(
        all_thirds_kernel,
        out_shape=jax.ShapeDtypeStruct((peers, depth, lat), views.dtype),
        in_specs=[SMEM, ANY],
        out_specs=ANY,
        scratch_shapes=[
            pltpu.SMEM((peers,), jnp.int32),
            pltpu.VMEM((depth, lat), views.dtype),
            pltpu.SemaphoreType.DMA((2,)),
        ],
        name="all_thirds",
    )(owners, views)


def group_count(peers):
    members = 1
    while peers % (2 * members) == 0 and members * members < peers:
        members *= 2
    return peers // members


def along_groups(rows):
    peers = lax.axis_size("join")
    members = peers // len(rows)
    line = [rows[0]]
    for k in range(1, len(rows)):
        line.append(
            lax.ppermute(rows[k], "join", [(i, (i + k * members) % peers) for i in range(peers)])
        )
    return line


def among_members(line):
    peers = lax.axis_size("join")
    members = peers // len(line)
    line = jnp.concatenate(line, axis=0)
    parts = [line]
    for m in range(1, members):
        parts.append(lax.ppermute(line, "join", [(i, i ^ m) for i in range(peers)]))
    return parts


def sources_of_parts(groups):
    peers = lax.axis_size("join")
    members = peers // groups
    here = lax.axis_index("join")
    at = jnp.arange(peers, dtype=jnp.int32)
    group = lax.rem(here // members + groups - lax.rem(at, groups), groups)
    return group * members + jnp.bitwise_xor(lax.rem(here, members), at // groups)


def ends_kernel(start, *refs):
    blocks, (out, staged, sems) = refs[:-3], refs[-3:]
    width = out.shape[1]
    copies, first = [], 0
    for k, block in enumerate(blocks):
        number = block.shape[0]
        held = staged.at[pl.ds(first, number)]
        rows = block.at[:, pl.ds(pl.multiple_of(start[0], TILE), width)]
        copies.append(
            (
                pltpu.make_async_copy(rows, held, sems.at[0, k]),
                pltpu.make_async_copy(held, out.at[pl.ds(first, number)], sems.at[1, k]),
            )
        )
        first += number
    for load, _ in copies:
        load.start()
    for load, store in copies:
        load.wait()
        store.start()
    for _, store in copies:
        store.wait()


def ends(blocks, start, width):
    if len(blocks) == 1:
        return lax.dynamic_slice_in_dim(blocks[0], start, width, axis=1)
    shape = (sum(block.shape[0] for block in blocks), width, blocks[0].shape[2])
    return pl.pallas_call(
        ends_kernel,
        out_shape=jax.ShapeDtypeStruct(shape, blocks[0].dtype),
        in_specs=[SMEM] + [ANY] * len(blocks),
        out_specs=ANY,
        scratch_shapes=[
            pltpu.VMEM(shape, blocks[0].dtype),
            pltpu.SemaphoreType.DMA((2, len(blocks))),
        ],
        name="ends",
    )(jnp.asarray(start, jnp.int32)[None], *blocks)


def halos(blocks, depth, width):
    count = lax.axis_size("view")
    if count == 1:
        return []
    if count == 2:
        sent = ends(blocks, jnp.where(lax.axis_index("view") == 0, depth - width, 0), width)
        return [lax.ppermute(sent, "view", [(0, 1), (1, 0)])]
    forward = [(i, i + 1) for i in range(count - 1)]
    backward = [(target, source) for source, target in forward]
    low = lax.ppermute(ends(blocks, depth - width, width), "view", forward)
    high = lax.ppermute(ends(blocks, 0, width), "view", backward)
    return [low, high]


def framed(block, sides, dim):
    if not sides:
        return block
    if len(sides) == 2:
        return jnp.concatenate([sides[0], block, sides[1]], axis=dim)
    (side,) = sides
    return jnp.where(
        lax.axis_index("view") == 0,
        jnp.concatenate([block, side], axis=dim),
        jnp.concatenate([side, block], axis=dim),
    )


def low_rows():
    count = lax.axis_size("view")
    if count == 2:
        return jnp.where(lax.axis_index("view") == 0, 0, H).astype(jnp.int32)
    return jnp.int32(0 if count == 1 else H)


def halo_rows(sweep):
    return VIEW_HALO - 2 * H * sweep


def piece_starts(depth, sweep):
    count = lax.axis_size("view")
    width = halo_rows(sweep)
    if count == 1:
        return [jnp.int32(0)]
    if count == 2:
        first = lax.axis_index("view") == 0
        return [jnp.where(first, 0, width), jnp.where(first, depth, 0)]
    return [jnp.int32(width), jnp.int32(0), jnp.int32(width + depth)]


def bands_kernel(shapes, shifts, taps_rows, *refs):
    width = taps_rows.shape[-1]
    nviews = taps_rows.shape[1]

    def band(which, v, shift, rows):
        spread = jnp.broadcast_to(taps_rows[which, v : v + 1, :], (rows, width))
        return pltpu.roll(pltpu.roll(spread, 0, 1, stride=1, stride_axis=0), shift, 1)

    at = 0
    for sweep, pieces in enumerate(shapes):
        forward, mirror = refs[2 * sweep], refs[2 * sweep + 1]
        columns, outs = forward.shape[2], mirror.shape[1]
        lane = lax.broadcasted_iota(jnp.int32, (outs, width), 1)
        for v in range(nviews):
            total = jnp.zeros((outs, width), jnp.float32)
            first = 0
            for piece, rows in enumerate(pieces):
                part = band(0, v, shifts[at + 2 * piece], rows)
                forward[v, first : first + rows] = part[:, :columns].astype(forward.dtype)
                inside = jnp.logical_and(lane >= first, lane < first + rows)
                total = jnp.where(inside, band(1, v, shifts[at + 2 * piece + 1], outs), total)
                first += rows
            mirror[v] = total[:, :first].astype(mirror.dtype)
        at += 2 * len(pieces)


def bands(kernel, depth, sides):
    nviews, taps = kernel.shape
    low = low_rows()
    frame = depth + sides * EST_HALO
    width = -(-(frame + 4 * H) // 128) * 128
    shapes, shifts, outs = [], [], []
    for sweep in range(ITERS):
        pieces = (depth,) + (halo_rows(sweep),) * sides
        first = 0
        for rows, start in zip(pieces, piece_starts(depth, sweep)):
            shifts.append(lax.rem(start + low - H + width, width))
            shifts.append(lax.rem(first - start + low - H + width, width))
            first += rows
        shapes.append(pieces)
        rows_in = frame - 2 * sides * H * sweep
        outs.append(jax.ShapeDtypeStruct((nviews, first, rows_in), jnp.bfloat16))
        outs.append(jax.ShapeDtypeStruct((nviews, rows_in - 2 * sides * H, first), jnp.bfloat16))
    rows = jnp.stack([kernel, kernel[:, ::-1]]).astype(jnp.float32)
    rows = jnp.pad(rows, ((0, 0), (0, 0), (0, width - taps)))
    return pl.pallas_call(
        functools.partial(bands_kernel, shapes),
        out_shape=outs,
        in_specs=[SMEM, VMEM],
        out_specs=[VMEM] * len(outs),
        cost_estimate=pl.CostEstimate(flops=10**11, bytes_accessed=0, transcendentals=0),
        name="bands",
    )(jnp.stack(shifts).astype(jnp.int32), rows)


def list_starts(peers):
    main, third = peers * MAIN + GROUP, peers + GROUP
    return 0, main, 2 * main, 2 * main + third, 2 * main + 2 * third, 2 * main + 3 * third


def plan_kernel(nviews, blocks, place, source, *refs):
    parts, (lists, any_crowded, tables, rows, scalars, sems) = refs[:-6], refs[-6:]
    per_part, depth, lat = parts[0].shape
    depth -= TILE
    peers = source.shape[0]
    blank = blocks * nviews
    main_slot, main_code, third_slot, third_source, third_code, numbers = list_starts(peers)
    loads = [
        pltpu.make_async_copy(
            part.at[:, pl.ds(depth, TILE)], tables.at[pl.ds(j * per_part, per_part)], sems.at[j]
        )
        for j, part in enumerate(parts)
    ]
    for load in loads:
        load.start()
    lists[numbers + 2] = place[1]
    for b in range(blocks):
        lists[numbers + 3 + b] = 0
    for load in loads:
        load.wait()
    at = lax.broadcasted_iota(jnp.int32, (peers, lat), 0)
    together = jnp.zeros((peers, lat), jnp.float32)
    for t in range(peers):
        row = jnp.broadcast_to(tables[t, :1].astype(jnp.float32), (peers, lat))
        together = jnp.where(at == t, row, together)
    rows[...] = together.astype(jnp.int32)
    copy = pltpu.make_async_copy(rows, scalars, sems.at[len(parts)])
    copy.start()
    copy.wait()

    def enlist(t, carry):
        in_main, in_third, crowded = carry
        for order in range(CAP):
            code = scalars[t, place[0] * CAP + order]
            valid = code >= 0

            @pl.when(valid)
            def _():
                at = numbers + 3 + code // nviews
                lists[at] = lists[at] + 1
                if order < MAIN:
                    lists[main_slot + in_main] = source[t] * MAIN + order
                    lists[main_code + in_main] = code
                else:
                    lists[third_slot + in_third] = t
                    lists[third_source + in_third] = source[t]
                    lists[third_code + in_third] = code

            if order < MAIN:
                in_main = in_main + valid.astype(jnp.int32)
            else:
                in_third = in_third + valid.astype(jnp.int32)
        return in_main, in_third, jnp.maximum(crowded, scalars[t, peers * CAP])

    zero = jnp.int32(0)
    in_main, in_third, crowded = lax.fori_loop(0, peers, enlist, (zero, zero, zero))
    lists[numbers] = in_main
    lists[numbers + 1] = in_third
    any_crowded[0] = crowded
    for more in range(GROUP - 1):
        lists[main_slot + in_main + more] = lists[main_slot]
        lists[main_code + in_main + more] = blank
        lists[third_code + in_third + more] = blank


def plan(parts, source, here, blocks, nviews):
    peers = source.shape[0]
    lat = parts[0].shape[-1]
    length = list_starts(peers)[-1] + 3 + blocks
    return pl.pallas_call(
        functools.partial(plan_kernel, nviews, blocks),
        out_shape=(
            jax.ShapeDtypeStruct((length,), jnp.int32),
            jax.ShapeDtypeStruct((1,), jnp.int32),
        ),
        in_specs=[SMEM] * 2 + [ANY] * len(parts),
        out_specs=(SMEM,) * 2,
        scratch_shapes=[
            pltpu.VMEM((peers, TILE, lat), parts[0].dtype),
            pltpu.VMEM((peers, lat), jnp.int32),
            pltpu.SMEM((peers, lat), jnp.int32),
            pltpu.SemaphoreType.DMA((len(parts) + 1,)),
        ],
        name="plan",
    )(jnp.stack([here, low_rows()]), source, *parts)


def deconvolve_kernel(starts, nparts, sides, guard, listed, main, est, *refs):
    main_slot, main_code, third_slot, third_code, numbers = starts
    parts, third_halo, refs = refs[:nparts], refs[nparts : nparts + sides], refs[nparts + sides :]
    number = 2 * ITERS + sides
    sources, out, refs = refs[:number], refs[number], refs[number + 1 :]
    copied, refs = refs[:number], refs[number:]
    bands_of, main_halo = copied[: 2 * ITERS], copied[2 * ITERS :]
    lists, held, recip, following, total, result, own_sems, held_sems, out_sems, lists_sem = refs
    blocks, depth, lat = out.shape
    nviews = bands_of[0].shape[0]
    per_part = parts[0].shape[0]
    own = [
        pltpu.make_async_copy(source, to, own_sems.at[k])
        for k, (source, to) in enumerate(zip(sources, copied))
    ]
    own[0].start()
    listing = pltpu.make_async_copy(listed, lists, lists_sem)
    listing.start()
    for copy in own[1:]:
        copy.start()
    listing.wait()

    mains, thirds = lists[numbers], lists[numbers + 1]
    low = pl.multiple_of(lists[numbers + 2], H)
    counts = [lists[numbers + 3 + b] for b in range(blocks)]
    def copies(p, part, at, slot):
        yield pltpu.make_async_copy(
            part.at[at, pl.ds(0, depth)], held.at[p, pl.ds(0, depth)], held_sems.at[p, 0]
        )
        for side, ref in enumerate(third_halo):
            rows = pl.ds(depth + side * VIEW_HALO, VIEW_HALO)
            yield pltpu.make_async_copy(ref.at[slot], held.at[p, rows], held_sems.at[p, 1 + side])

    @pl.loop(0, thirds)
    def _(p):
        slot = lists[third_slot + p]
        for j, part in enumerate(parts):

            @pl.when(jnp.logical_and(slot >= j * per_part, slot < (j + 1) * per_part))
            def _():
                for copy in copies(p, part, slot - j * per_part, slot):
                    copy.start()

    @pl.loop(thirds, (thirds + (GROUP - 1)) // GROUP * GROUP)
    def _(p):
        held[p] = jnp.zeros(held.shape[1:], held.dtype)

    recip[blocks * nviews] = jnp.zeros(recip.shape[1:], recip.dtype)
    stores = []
    for sweep in range(ITERS):
        current = est if sweep == 0 else following
        forward, mirror = bands_of[2 * sweep], bands_of[2 * sweep + 1]
        next_rows, view_rows = mirror.shape[1], mirror.shape[2]
        side_rows = halo_rows(sweep)
        next_at = pl.multiple_of(2 * low, 2 * H)
        halo_at = [pl.multiple_of(2 * sweep * low, 2 * H), 0]
        own[2 * sweep].wait()
        for b in range(blocks):
            rounded = current[b, : forward.shape[2]].astype(jnp.bfloat16)
            for v in range(nviews):
                blurred = jnp.dot(forward[v], rounded, preferred_element_type=jnp.float32)
                inverse = 1.0 / blurred
                if guard:
                    inverse = jnp.where(blurred > 0, inverse, 0.0)
                recip[b * nviews + v, :view_rows] = inverse

        total[:, :next_rows] = jnp.zeros((blocks + 1, next_rows, lat), jnp.float32)

        def main_rows(p):
            slot = lists[main_slot + p]
            rows = [main[slot]]
            for side, ref in enumerate(main_halo):
                rows.append(ref[slot, pl.ds(halo_at[side], side_rows)])
            return rows

        def third_rows(p):
            rows = [held[p, :depth]]
            for side in range(sides):
                at = depth + side * VIEW_HALO + halo_at[side]
                rows.append(held[p, pl.ds(pl.multiple_of(at, H), side_rows)])
            return rows

        def add(number, rows_of, code_at):
            @pl.loop(0, (number + (GROUP - 1)) // GROUP)
            def _(group):
                gained = []
                for member in range(GROUP):
                    p = group * GROUP + member
                    code = lists[code_at + p]
                    b = code // nviews
                    pieces, first = [], 0
                    for rows in rows_of(p):
                        last = first + rows.shape[0]
                        quotient = rows.astype(jnp.float32) * recip[code, first:last]
                        pieces.append(quotient.astype(jnp.bfloat16))
                        first = last
                    part = jnp.dot(
                        mirror[code - b * nviews],
                        jnp.concatenate(pieces, axis=0),
                        preferred_element_type=jnp.float32,
                    )
                    gained.append((b, part))
                for b, part in gained:
                    total[b, :next_rows] += part

        own[2 * sweep + 1].wait()
        if sweep == 0:
            for copy in own[2 * ITERS :]:
                copy.wait()
        add(mains, main_rows, main_code)
        if sweep == 0:

            @pl.loop(0, thirds)
            def _(p):
                for copy in copies(p, parts[0], 0, 0):
                    copy.wait()

        add(thirds, third_rows, third_code)
        for b in range(blocks):
            average = total[b, :next_rows] / jnp.maximum(counts[b], 1).astype(jnp.float32)
            factor = jnp.where(counts[b] > 0, average, 1.0)
            updated = current[b, pl.ds(next_at, next_rows)] * factor
            if sweep < ITERS - 1:
                following[b, :next_rows] = updated
            else:
                result[b] = updated
                store = pltpu.make_async_copy(result.at[b], out.at[b], out_sems.at[b])
                store.start()
                stores.append(store)
    for store in stores:
        store.wait()


def deconvolve(lists, starts, main, parts, main_halo, third_halo, est, matrices, depth, guard):
    blocks, frame, lat = est.shape
    nviews, view_rows = matrices[0].shape[:2]
    sides = len(main_halo)
    thirds = parts[0].shape[0] * len(parts) + GROUP
    following = (frame - 2 * sides * H, lat)
    copied = [*matrices, *main_halo]
    in_place = [*parts, *third_halo, *copied]
    return pl.pallas_call(
        functools.partial(deconvolve_kernel, starts, len(parts), sides, guard),
        out_shape=pltpu.HBM((blocks, depth, lat), jnp.float32),
        in_specs=[ANY] + [VMEM] * 2 + [ANY] * len(in_place),
        out_specs=HBM,
        scratch_shapes=[pltpu.VMEM(array.shape, array.dtype) for array in copied]
        + [
            pltpu.SMEM(lists.shape, lists.dtype),
            pltpu.VMEM((thirds, view_rows, lat), jnp.bfloat16),
            pltpu.VMEM((blocks * nviews + 1, view_rows, lat), jnp.float32),
            pltpu.VMEM((blocks, *following), jnp.float32),
            pltpu.VMEM((blocks + 1, *following), jnp.float32),
            pltpu.VMEM((blocks, depth, lat), jnp.float32),
            pltpu.SemaphoreType.DMA((len(copied),)),
            pltpu.SemaphoreType.DMA((thirds, 1 + sides)),
            pltpu.SemaphoreType.DMA((blocks,)),
            pltpu.SemaphoreType.DMA,
        ],
        compiler_params=pltpu.CompilerParams(vmem_limit_bytes=24 * 1024 * 1024),
        name="deconvolve",
    )(lists, main, est, *in_place)


def local(estimate, views, owners, local_blocks, psf):
    blocks, depth, lat = estimate.shape
    nviews = views.shape[1]
    peers = lax.axis_size("join")
    groups = group_count(peers)
    here = lax.axis_index("join").astype(jnp.int32)
    normed = psf / jnp.sum(psf, axis=1, keepdims=True)
    kernel = normed.astype(jnp.bfloat16)

    packed, *rows = pack(
        views, owners, local_blocks, (here // (peers // groups))[None], peers, groups
    )
    line = along_groups(rows)
    arrived = lax.all_to_all(
        packed.reshape(peers, MAIN, depth, lat), "join", split_axis=0, concat_axis=0, tiled=True
    ).reshape(peers * MAIN, depth, lat)

    parts = among_members(line)
    source = sources_of_parts(groups)
    kernel, estimate, line = lax.optimization_barrier((kernel, estimate, line))
    est_halos = halos([estimate], depth, EST_HALO)
    est = framed(estimate, est_halos, 1)
    matrices = bands(kernel, depth, len(est_halos))
    parts, source, est, matrices = lax.optimization_barrier((parts, source, est, matrices))
    third_halo = halos(parts, depth, VIEW_HALO)
    planned = plan(parts, source, here, blocks, nviews)
    arrived, parts, third_halo, planned, est, matrices = lax.optimization_barrier(
        (arrived, parts, third_halo, planned, est, matrices)
    )
    lists, any_crowded = planned
    main_slot, main_code, third_slot, third_source, third_code, numbers = list_starts(peers)

    main_halo = halos([arrived], depth, VIEW_HALO)
    guard = lax.axis_size("view") > 2

    def finish(third_at, thirds, third_halo):
        return deconvolve(
            lists,
            (main_slot, main_code, third_at, third_code, numbers),
            arrived,
            thirds,
            main_halo,
            third_halo,
            est,
            matrices,
            depth,
            guard,
        )

    def fallback():
        sent = pack_all_thirds(views, owners, peers)
        thirds = lax.all_to_all(sent, "join", split_axis=0, concat_axis=0, tiled=True)
        return finish(third_source, [thirds], halos([thirds], depth, VIEW_HALO))

    return lax.cond(
        any_crowded[0] > 0, fallback, lambda: finish(third_slot, parts, third_halo)
    )


def solution(mesh):
    in_specs = (
        P("join", "view", None),
        P("join", None, "view", None),
        P("join", None),
        P("join", None),
        P(),
    )
    out_specs = P("join", "view", None)
    return jax.shard_map(local, mesh=mesh, in_specs=in_specs, out_specs=out_specs, check_vma=False)
```

```python
import functools

import jax
import jax.numpy as jnp
from jax import lax
from jax.experimental import pallas as pl
from jax.experimental.pallas import tpu as pltpu
from jax.sharding import PartitionSpec as P

H = 16
CAP = 3
MAIN = 2
ITERS = 2
GROUP = 16
TILE = 16
EST_HALO = 2 * ITERS * H
VIEW_HALO = EST_HALO - H

SMEM = pl.BlockSpec(memory_space=pltpu.SMEM)
VMEM = pl.BlockSpec(memory_space=pltpu.VMEM)
ANY = pl.BlockSpec(memory_space=pl.ANY)
HBM = pl.BlockSpec(memory_space=pltpu.HBM)


def pack_kernel(owners, blocks_of, here, views, main, *refs):
    rows, (table, seen, taken, staged, table_rows, in_sems, out_sems, table_sems) = refs[:-8], refs[-8:]
    blocks, nviews, depth, lat = views.shape
    peers, groups = seen.shape[0], len(rows)
    members = peers // groups
    pairs = [(i, v) for i in range(blocks) for v in range(nviews)]
    loads = [
        pltpu.make_async_copy(views.at[i, v], staged.at[i, v], in_sems.at[i, v]) for i, v in pairs
    ]
    for load in loads:
        load.start()

    @pl.loop(0, peers)
    def _(peer):
        seen[peer] = 0

    for group in range(groups):
        taken[group] = 0

    @pl.loop(0, peers * CAP)
    def _(slot):
        table[slot] = -1

    table[peers * CAP] = 0
    stores = []
    for (i, v), load in zip(pairs, loads):
        owner = owners[i, v]
        order = seen[owner]
        seen[owner] = order + 1
        table[owner * CAP + order] = blocks_of[i, v] * nviews + v
        away = lax.rem(owner // members + groups - here[0], groups)
        in_main = order < MAIN
        in_rows = jnp.logical_and(jnp.logical_not(in_main), taken[away] == 0)
        load.wait()

        @pl.when(in_main)
        def _():
            pltpu.make_async_copy(
                staged.at[i, v], main.at[owner * MAIN + order], out_sems.at[i, v]
            ).start()

        @pl.when(jnp.logical_not(in_main))
        def _():
            table[peers * CAP] = jnp.where(in_rows, table[peers * CAP], 1)
            for k in range(groups):

                @pl.when(jnp.logical_and(in_rows, away == k))
                def _():
                    taken[k] = 1
                    pltpu.make_async_copy(
                        staged.at[i, v], rows[k].at[0, pl.ds(0, depth)], out_sems.at[i, v]
                    ).start()

        stores.append((i, v, jnp.logical_or(in_main, in_rows)))

    lane = lax.broadcasted_iota(jnp.int32, (TILE, lat), 1)
    row = jnp.full((TILE, lat), -1, jnp.int32)
    for slot in range(peers * CAP + 1):
        row = jnp.where(lane == slot, table[slot], row)
    table_rows[...] = row.astype(jnp.float32).astype(table_rows.dtype)
    table_stores = [
        pltpu.make_async_copy(table_rows, rows[k].at[0, pl.ds(depth, TILE)], table_sems.at[k])
        for k in range(groups)
    ]
    for store in table_stores:
        store.start()
    for i, v, stored in stores:

        @pl.when(stored)
        def _():
            pltpu.make_async_copy(staged.at[i, v], main.at[0], out_sems.at[i, v]).wait()

    for store in table_stores:
        store.wait()


def pack(views, owners, blocks_of, here, peers, groups):
    blocks, nviews, depth, lat = views.shape
    assert peers * CAP < lat
    return pl.pallas_call(
        pack_kernel,
        out_shape=(jax.ShapeDtypeStruct((peers * MAIN, depth, lat), views.dtype),)
        + (jax.ShapeDtypeStruct((1, depth + TILE, lat), views.dtype),) * groups,
        in_specs=[SMEM, SMEM, SMEM, ANY],
        out_specs=(ANY,) * (1 + groups),
        scratch_shapes=[
            pltpu.SMEM((peers * CAP + 1,), jnp.int32),
            pltpu.SMEM((peers,), jnp.int32),
            pltpu.SMEM((groups,), jnp.int32),
            pltpu.VMEM(views.shape, views.dtype),
            pltpu.VMEM((TILE, lat), views.dtype),
            pltpu.SemaphoreType.DMA((blocks, nviews)),
            pltpu.SemaphoreType.DMA((blocks, nviews)),
            pltpu.SemaphoreType.DMA((groups,)),
        ],
        name="pack",
    )(owners, blocks_of, here, views)


def all_thirds_kernel(owners, views, out, seen, staged, sems):
    blocks, nviews = views.shape[0], views.shape[1]

    @pl.loop(0, out.shape[0])
    def _(peer):
        seen[peer] = 0

    for i in range(blocks):
        for v in range(nviews):
            owner = owners[i, v]
            order = seen[owner]
            seen[owner] = order + 1

            @pl.when(order >= MAIN)
            def _():
                load = pltpu.make_async_copy(views.at[i, v], staged, sems.at[0])
                load.start()
                load.wait()
                store = pltpu.make_async_copy(staged, out.at[owner], sems.at[1])
                store.start()
                store.wait()


def pack_all_thirds(views, owners, peers):
    depth, lat = views.shape[2:]
    return pl.pallas_call(
        all_thirds_kernel,
        out_shape=jax.ShapeDtypeStruct((peers, depth, lat), views.dtype),
        in_specs=[SMEM, ANY],
        out_specs=ANY,
        scratch_shapes=[
            pltpu.SMEM((peers,), jnp.int32),
            pltpu.VMEM((depth, lat), views.dtype),
            pltpu.SemaphoreType.DMA((2,)),
        ],
        name="all_thirds",
    )(owners, views)


def group_count(peers):
    members = 1
    while peers % (2 * members) == 0 and members * members < peers:
        members *= 2
    return peers // members


def along_groups(rows):
    peers = lax.axis_size("join")
    members = peers // len(rows)
    line = [rows[0]]
    for k in range(1, len(rows)):
        line.append(
            lax.ppermute(rows[k], "join", [(i, (i + k * members) % peers) for i in range(peers)])
        )
    return line


def among_members(line):
    peers = lax.axis_size("join")
    members = peers // len(line)
    line = jnp.concatenate(line, axis=0)
    parts = [line]
    for m in range(1, members):
        parts.append(lax.ppermute(line, "join", [(i, i ^ m) for i in range(peers)]))
    return parts


def sources_of_parts(groups):
    peers = lax.axis_size("join")
    members = peers // groups
    here = lax.axis_index("join")
    at = jnp.arange(peers, dtype=jnp.int32)
    group = lax.rem(here // members + groups - lax.rem(at, groups), groups)
    return group * members + jnp.bitwise_xor(lax.rem(here, members), at // groups)


def ends_kernel(start, *refs):
    blocks, (out, staged, sems) = refs[:-3], refs[-3:]
    width = out.shape[1]
    copies, first = [], 0
    for k, block in enumerate(blocks):
        number = block.shape[0]
        held = staged.at[pl.ds(first, number)]
        rows = block.at[:, pl.ds(pl.multiple_of(start[0], TILE), width)]
        copies.append(
            (
                pltpu.make_async_copy(rows, held, sems.at[0, k]),
                pltpu.make_async_copy(held, out.at[pl.ds(first, number)], sems.at[1, k]),
            )
        )
        first += number
    for load, _ in copies:
        load.start()
    for load, store in copies:
        load.wait()
        store.start()
    for _, store in copies:
        store.wait()


def ends(blocks, start, width):
    if len(blocks) == 1:
        return lax.dynamic_slice_in_dim(blocks[0], start, width, axis=1)
    shape = (sum(block.shape[0] for block in blocks), width, blocks[0].shape[2])
    return pl.pallas_call(
        ends_kernel,
        out_shape=jax.ShapeDtypeStruct(shape, blocks[0].dtype),
        in_specs=[SMEM] + [ANY] * len(blocks),
        out_specs=ANY,
        scratch_shapes=[
            pltpu.VMEM(shape, blocks[0].dtype),
            pltpu.SemaphoreType.DMA((2, len(blocks))),
        ],
        name="ends",
    )(jnp.asarray(start, jnp.int32)[None], *blocks)


def halos(blocks, depth, width):
    count = lax.axis_size("view")
    if count == 1:
        return []
    if count == 2:
        sent = ends(blocks, jnp.where(lax.axis_index("view") == 0, depth - width, 0), width)
        return [lax.ppermute(sent, "view", [(0, 1), (1, 0)])]
    forward = [(i, i + 1) for i in range(count - 1)]
    backward = [(target, source) for source, target in forward]
    low = lax.ppermute(ends(blocks, depth - width, width), "view", forward)
    high = lax.ppermute(ends(blocks, 0, width), "view", backward)
    return [low, high]


def framed(block, sides, dim):
    if not sides:
        return block
    if len(sides) == 2:
        return jnp.concatenate([sides[0], block, sides[1]], axis=dim)
    (side,) = sides
    return jnp.where(
        lax.axis_index("view") == 0,
        jnp.concatenate([block, side], axis=dim),
        jnp.concatenate([side, block], axis=dim),
    )


def low_rows():
    count = lax.axis_size("view")
    if count == 2:
        return jnp.where(lax.axis_index("view") == 0, 0, H).astype(jnp.int32)
    return jnp.int32(0 if count == 1 else H)


def halo_rows(sweep):
    return VIEW_HALO - 2 * H * sweep


def piece_starts(depth, sweep):
    count = lax.axis_size("view")
    width = halo_rows(sweep)
    if count == 1:
        return [jnp.int32(0)]
    if count == 2:
        first = lax.axis_index("view") == 0
        return [jnp.where(first, 0, width), jnp.where(first, depth, 0)]
    return [jnp.int32(width), jnp.int32(0), jnp.int32(width + depth)]


def bands_kernel(shapes, shifts, taps_rows, *refs):
    width = taps_rows.shape[-1]
    nviews = taps_rows.shape[1]

    def band(which, v, shift, rows):
        spread = jnp.broadcast_to(taps_rows[which, v : v + 1, :], (rows, width))
        return pltpu.roll(pltpu.roll(spread, 0, 1, stride=1, stride_axis=0), shift, 1)

    at = 0
    for sweep, pieces in enumerate(shapes):
        forward, mirror = refs[2 * sweep], refs[2 * sweep + 1]
        columns, outs = forward.shape[2], mirror.shape[1]
        lane = lax.broadcasted_iota(jnp.int32, (outs, width), 1)
        for v in range(nviews):
            total = jnp.zeros((outs, width), jnp.float32)
            first = 0
            for piece, rows in enumerate(pieces):
                part = band(0, v, shifts[at + 2 * piece], rows)
                forward[v, first : first + rows] = part[:, :columns].astype(forward.dtype)
                inside = jnp.logical_and(lane >= first, lane < first + rows)
                total = jnp.where(inside, band(1, v, shifts[at + 2 * piece + 1], outs), total)
                first += rows
            mirror[v] = total[:, :first].astype(mirror.dtype)
        at += 2 * len(pieces)


def bands(kernel, depth, sides):
    nviews, taps = kernel.shape
    low = low_rows()
    frame = depth + sides * EST_HALO
    width = -(-(frame + 4 * H) // 128) * 128
    shapes, shifts, outs = [], [], []
    for sweep in range(ITERS):
        pieces = (depth,) + (halo_rows(sweep),) * sides
        first = 0
        for rows, start in zip(pieces, piece_starts(depth, sweep)):
            shifts.append(lax.rem(start + low - H + width, width))
            shifts.append(lax.rem(first - start + low - H + width, width))
            first += rows
        shapes.append(pieces)
        rows_in = frame - 2 * sides * H * sweep
        outs.append(jax.ShapeDtypeStruct((nviews, first, rows_in), jnp.bfloat16))
        outs.append(jax.ShapeDtypeStruct((nviews, rows_in - 2 * sides * H, first), jnp.bfloat16))
    rows = jnp.stack([kernel, kernel[:, ::-1]]).astype(jnp.float32)
    rows = jnp.pad(rows, ((0, 0), (0, 0), (0, width - taps)))
    return pl.pallas_call(
        functools.partial(bands_kernel, shapes),
        out_shape=outs,
        in_specs=[SMEM, VMEM],
        out_specs=[VMEM] * len(outs),
        cost_estimate=pl.CostEstimate(flops=10**11, bytes_accessed=0, transcendentals=0),
        name="bands",
    )(jnp.stack(shifts).astype(jnp.int32), rows)


def list_starts(peers):
    main, third = peers * MAIN + GROUP, peers + GROUP
    return 0, main, 2 * main, 2 * main + third, 2 * main + 2 * third, 2 * main + 3 * third


def plan_kernel(nviews, blocks, place, source, *refs):
    parts, (lists, any_crowded, tables, rows, scalars, sems) = refs[:-6], refs[-6:]
    per_part, depth, lat = parts[0].shape
    depth -= TILE
    peers = source.shape[0]
    blank = blocks * nviews
    main_slot, main_code, third_slot, third_source, third_code, numbers = list_starts(peers)
    loads = [
        pltpu.make_async_copy(
            part.at[:, pl.ds(depth, TILE)], tables.at[pl.ds(j * per_part, per_part)], sems.at[j]
        )
        for j, part in enumerate(parts)
    ]
    for load in loads:
        load.start()
    lists[numbers + 2] = place[1]
    for b in range(blocks):
        lists[numbers + 3 + b] = 0
    for load in loads:
        load.wait()
    at = lax.broadcasted_iota(jnp.int32, (peers, lat), 0)
    together = jnp.zeros((peers, lat), jnp.float32)
    for t in range(peers):
        row = jnp.broadcast_to(tables[t, :1].astype(jnp.float32), (peers, lat))
        together = jnp.where(at == t, row, together)
    rows[...] = together.astype(jnp.int32)
    copy = pltpu.make_async_copy(rows, scalars, sems.at[len(parts)])
    copy.start()
    copy.wait()

    def enlist(t, carry):
        in_main, in_third, crowded = carry
        for order in range(CAP):
            code = scalars[t, place[0] * CAP + order]
            valid = code >= 0

            @pl.when(valid)
            def _():
                at = numbers + 3 + code // nviews
                lists[at] = lists[at] + 1
                if order < MAIN:
                    lists[main_slot + in_main] = source[t] * MAIN + order
                    lists[main_code + in_main] = code
                else:
                    lists[third_slot + in_third] = t
                    lists[third_source + in_third] = source[t]
                    lists[third_code + in_third] = code

            if order < MAIN:
                in_main = in_main + valid.astype(jnp.int32)
            else:
                in_third = in_third + valid.astype(jnp.int32)
        return in_main, in_third, jnp.maximum(crowded, scalars[t, peers * CAP])

    zero = jnp.int32(0)
    in_main, in_third, crowded = lax.fori_loop(0, peers, enlist, (zero, zero, zero))
    lists[numbers] = in_main
    lists[numbers + 1] = in_third
    any_crowded[0] = crowded
    for more in range(GROUP - 1):
        lists[main_slot + in_main + more] = lists[main_slot]
        lists[main_code + in_main + more] = blank
        lists[third_slot + in_third + more] = lists[third_slot]
        lists[third_source + in_third + more] = lists[third_source]
        lists[third_code + in_third + more] = blank


def plan(parts, source, here, blocks, nviews):
    peers = source.shape[0]
    lat = parts[0].shape[-1]
    length = list_starts(peers)[-1] + 3 + blocks
    return pl.pallas_call(
        functools.partial(plan_kernel, nviews, blocks),
        out_shape=(
            jax.ShapeDtypeStruct((length,), jnp.int32),
            jax.ShapeDtypeStruct((1,), jnp.int32),
        ),
        in_specs=[SMEM] * 2 + [ANY] * len(parts),
        out_specs=(SMEM,) * 2,
        scratch_shapes=[
            pltpu.VMEM((peers, TILE, lat), parts[0].dtype),
            pltpu.VMEM((peers, lat), jnp.int32),
            pltpu.SMEM((peers, lat), jnp.int32),
            pltpu.SemaphoreType.DMA((len(parts) + 1,)),
        ],
        name="plan",
    )(jnp.stack([here, low_rows()]), source, *parts)


def deconvolve_kernel(starts, nparts, sides, guard, listed, main, est, *refs):
    main_slot, main_code, third_slot, third_code, numbers = starts
    parts, third_halo, refs = refs[:nparts], refs[nparts : nparts + sides], refs[nparts + sides :]
    number = 2 * ITERS + sides
    sources, out, refs = refs[:number], refs[number], refs[number + 1 :]
    copied, refs = refs[:number], refs[number:]
    bands_of, main_halo = copied[: 2 * ITERS], copied[2 * ITERS :]
    lists, held, *refs = refs
    held_halo, refs = refs[:sides], refs[sides:]
    recip, following, total, result, own_sems, held_sems, out_sems, lists_sem = refs
    blocks, depth, lat = out.shape
    nviews = bands_of[0].shape[0]
    own = [
        pltpu.make_async_copy(source, to, own_sems.at[k])
        for k, (source, to) in enumerate(zip(sources, copied))
    ]
    own[0].start()
    listing = pltpu.make_async_copy(listed, lists, lists_sem)
    listing.start()
    for copy in own[1:]:
        copy.start()
    number, part_rows = parts[0].shape[0], parts[0].shape[1]
    third_copies = [
        pltpu.make_async_copy(
            part, held.at[pl.ds(j * number, number), pl.ds(0, part_rows)], held_sems.at[j]
        )
        for j, part in enumerate(parts)
    ] + [
        pltpu.make_async_copy(ref, to, held_sems.at[nparts + side])
        for side, (ref, to) in enumerate(zip(third_halo, held_halo))
    ]
    recip[blocks * nviews] = jnp.zeros(recip.shape[1:], recip.dtype)
    stores = []
    for sweep in range(ITERS):
        current = est if sweep == 0 else following
        forward, mirror = bands_of[2 * sweep], bands_of[2 * sweep + 1]
        next_rows, view_rows = mirror.shape[1], mirror.shape[2]
        side_rows = halo_rows(sweep)
        own[2 * sweep].wait()
        for b in range(blocks):
            rounded = current[b, : forward.shape[2]].astype(jnp.bfloat16)
            for v in range(nviews):
                blurred = jnp.dot(forward[v], rounded, preferred_element_type=jnp.float32)
                inverse = 1.0 / blurred
                if guard:
                    inverse = jnp.where(blurred > 0, inverse, 0.0)
                recip[b * nviews + v, :view_rows] = inverse

        if sweep == 0:
            listing.wait()
            mains, thirds = lists[numbers], lists[numbers + 1]
            low = pl.multiple_of(lists[numbers + 2], H)
            counts = [lists[numbers + 3 + b] for b in range(blocks)]

            @pl.when(thirds > 0)
            def _():
                for copy in third_copies:
                    copy.start()

        next_at = pl.multiple_of(2 * low, 2 * H)
        halo_at = [pl.multiple_of(2 * sweep * low, 2 * H), 0]
        total[:, :next_rows] = jnp.zeros((blocks + 1, next_rows, lat), jnp.float32)

        def main_rows(p):
            slot = lists[main_slot + p]
            rows = [main[slot]]
            for side, ref in enumerate(main_halo):
                rows.append(ref[slot, pl.ds(halo_at[side], side_rows)])
            return rows

        def third_rows(p):
            slot = lists[third_slot + p]
            rows = [held[slot, :depth]]
            for side, ref in enumerate(held_halo):
                rows.append(ref[slot, pl.ds(halo_at[side], side_rows)])
            return rows

        def add(number, rows_of, code_at):
            @pl.loop(0, (number + (GROUP - 1)) // GROUP)
            def _(group):
                gained = []
                for member in range(GROUP):
                    p = group * GROUP + member
                    code = lists[code_at + p]
                    b = code // nviews
                    pieces, first = [], 0
                    for rows in rows_of(p):
                        last = first + rows.shape[0]
                        quotient = rows.astype(jnp.float32) * recip[code, first:last]
                        pieces.append(quotient.astype(jnp.bfloat16))
                        first = last
                    part = jnp.dot(
                        mirror[code - b * nviews],
                        jnp.concatenate(pieces, axis=0),
                        preferred_element_type=jnp.float32,
                    )
                    gained.append((b, part))
                for b, part in gained:
                    total[b, :next_rows] += part

        own[2 * sweep + 1].wait()
        if sweep == 0:
            for copy in own[2 * ITERS :]:
                copy.wait()
        add(mains, main_rows, main_code)
        if sweep == 0:

            @pl.when(thirds > 0)
            def _():
                for copy in third_copies:
                    copy.wait()

        add(thirds, third_rows, third_code)
        for b in range(blocks):
            average = total[b, :next_rows] / jnp.maximum(counts[b], 1).astype(jnp.float32)
            factor = jnp.where(counts[b] > 0, average, 1.0)
            updated = current[b, pl.ds(next_at, next_rows)] * factor
            if sweep < ITERS - 1:
                following[b, :next_rows] = updated
            else:
                result[b] = updated
                store = pltpu.make_async_copy(result.at[b], out.at[b], out_sems.at[b])
                store.start()
                stores.append(store)
    for store in stores:
        store.wait()


def deconvolve(lists, starts, main, parts, main_halo, third_halo, est, matrices, depth, guard):
    blocks, frame, lat = est.shape
    nviews, view_rows = matrices[0].shape[:2]
    sides = len(main_halo)
    following = (frame - 2 * sides * H, lat)
    third_halo_shape = (len(parts) * parts[0].shape[0], VIEW_HALO, lat)
    copied = [*matrices, *main_halo]
    in_place = [*parts, *third_halo, *copied]
    return pl.pallas_call(
        functools.partial(deconvolve_kernel, starts, len(parts), sides, guard),
        out_shape=pltpu.HBM((blocks, depth, lat), jnp.float32),
        in_specs=[ANY] + [VMEM] * 2 + [ANY] * len(in_place),
        out_specs=HBM,
        scratch_shapes=[pltpu.VMEM(array.shape, array.dtype) for array in copied]
        + [
            pltpu.SMEM(lists.shape, lists.dtype),
            pltpu.VMEM((third_halo_shape[0], depth + TILE, lat), main.dtype),
        ]
        + [pltpu.VMEM(third_halo_shape, main.dtype)] * sides
        + [
            pltpu.VMEM((blocks * nviews + 1, view_rows, lat), jnp.float32),
            pltpu.VMEM((blocks, *following), jnp.float32),
            pltpu.VMEM((blocks + 1, *following), jnp.float32),
            pltpu.VMEM((blocks, depth, lat), jnp.float32),
            pltpu.SemaphoreType.DMA((len(copied),)),
            pltpu.SemaphoreType.DMA((len(parts) + sides,)),
            pltpu.SemaphoreType.DMA((blocks,)),
            pltpu.SemaphoreType.DMA,
        ],
        compiler_params=pltpu.CompilerParams(vmem_limit_bytes=24 * 1024 * 1024),
        name="deconvolve",
    )(lists, main, est, *in_place)


def local(estimate, views, owners, local_blocks, psf):
    blocks, depth, lat = estimate.shape
    nviews = views.shape[1]
    peers = lax.axis_size("join")
    groups = group_count(peers)
    here = lax.axis_index("join").astype(jnp.int32)
    normed = psf / jnp.sum(psf, axis=1, keepdims=True)
    kernel = normed.astype(jnp.bfloat16)

    packed, *rows = pack(
        views, owners, local_blocks, (here // (peers // groups))[None], peers, groups
    )
    line = along_groups(rows)
    arrived = lax.all_to_all(
        packed.reshape(peers, MAIN, depth, lat), "join", split_axis=0, concat_axis=0, tiled=True
    ).reshape(peers * MAIN, depth, lat)

    parts = among_members(line)
    source = sources_of_parts(groups)
    kernel, estimate, line = lax.optimization_barrier((kernel, estimate, line))
    est_halos = halos([estimate], depth, EST_HALO)
    est = framed(estimate, est_halos, 1)
    matrices = bands(kernel, depth, len(est_halos))
    parts, source, est, matrices = lax.optimization_barrier((parts, source, est, matrices))
    third_halo = halos(parts, depth, VIEW_HALO)
    planned = plan(parts, source, here, blocks, nviews)
    arrived, parts, third_halo, planned, est, matrices = lax.optimization_barrier(
        (arrived, parts, third_halo, planned, est, matrices)
    )
    lists, any_crowded = planned
    main_slot, main_code, third_slot, third_source, third_code, numbers = list_starts(peers)

    main_halo = halos([arrived], depth, VIEW_HALO)
    guard = lax.axis_size("view") > 2

    def finish(third_at, thirds, third_halo):
        return deconvolve(
            lists,
            (main_slot, main_code, third_at, third_code, numbers),
            arrived,
            thirds,
            main_halo,
            third_halo,
            est,
            matrices,
            depth,
            guard,
        )

    def fallback():
        sent = pack_all_thirds(views, owners, peers)
        thirds = lax.all_to_all(sent, "join", split_axis=0, concat_axis=0, tiled=True)
        return finish(third_source, [thirds], halos([thirds], depth, VIEW_HALO))

    return lax.cond(
        any_crowded[0] > 0, fallback, lambda: finish(third_slot, parts, third_halo)
    )


def solution(mesh):
    in_specs = (
        P("join", "view", None),
        P("join", None, "view", None),
        P("join", None),
        P("join", None),
        P(),
    )
    out_specs = P("join", "view", None)
    return jax.shard_map(local, mesh=mesh, in_specs=in_specs, out_specs=out_specs, check_vma=False)
```

```python
import functools

import jax
import jax.numpy as jnp
from jax import lax
from jax.experimental import pallas as pl
from jax.experimental.pallas import tpu as pltpu
from jax.sharding import PartitionSpec as P

H = 16
CAP = 3
MAIN = 2
ITERS = 2
GROUP = 32
SMALL = 16
TILE = 16
EST_HALO = 2 * ITERS * H
VIEW_HALO = EST_HALO - H

SMEM = pl.BlockSpec(memory_space=pltpu.SMEM)
VMEM = pl.BlockSpec(memory_space=pltpu.VMEM)
ANY = pl.BlockSpec(memory_space=pl.ANY)
HBM = pl.BlockSpec(memory_space=pltpu.HBM)


def pack_kernel(owners, blocks_of, here, views, main, *refs):
    rows, (table, seen, taken, staged, table_rows, in_sems, out_sems, table_sems) = refs[:-8], refs[-8:]
    blocks, nviews, depth, lat = views.shape
    peers, groups = seen.shape[0], len(rows)
    members = peers // groups
    pairs = [(i, v) for i in range(blocks) for v in range(nviews)]
    loads = [
        pltpu.make_async_copy(views.at[i, v], staged.at[i, v], in_sems.at[i, v]) for i, v in pairs
    ]
    for load in loads:
        load.start()

    @pl.loop(0, peers)
    def _(peer):
        seen[peer] = 0

    for group in range(groups):
        taken[group] = 0

    @pl.loop(0, peers * CAP)
    def _(slot):
        table[slot] = -1

    table[peers * CAP] = 0
    stores = []
    for (i, v), load in zip(pairs, loads):
        owner = owners[i, v]
        order = seen[owner]
        seen[owner] = order + 1
        table[owner * CAP + order] = blocks_of[i, v] * nviews + v
        away = lax.rem(owner // members + groups - here[0], groups)
        in_main = order < MAIN
        in_rows = jnp.logical_and(jnp.logical_not(in_main), taken[away] == 0)
        load.wait()

        @pl.when(in_main)
        def _():
            pltpu.make_async_copy(
                staged.at[i, v], main.at[owner * MAIN + order], out_sems.at[i, v]
            ).start()

        @pl.when(jnp.logical_not(in_main))
        def _():
            table[peers * CAP] = jnp.where(in_rows, table[peers * CAP], 1)
            for k in range(groups):

                @pl.when(jnp.logical_and(in_rows, away == k))
                def _():
                    taken[k] = 1
                    pltpu.make_async_copy(
                        staged.at[i, v], rows[k].at[0, pl.ds(0, depth)], out_sems.at[i, v]
                    ).start()

        stores.append((i, v, jnp.logical_or(in_main, in_rows)))

    lane = lax.broadcasted_iota(jnp.int32, (TILE, lat), 1)
    row = jnp.full((TILE, lat), -1, jnp.int32)
    for slot in range(peers * CAP + 1):
        row = jnp.where(lane == slot, table[slot], row)
    table_rows[...] = row.astype(jnp.float32).astype(table_rows.dtype)
    table_stores = [
        pltpu.make_async_copy(table_rows, rows[k].at[0, pl.ds(depth, TILE)], table_sems.at[k])
        for k in range(groups)
    ]
    for store in table_stores:
        store.start()
    for i, v, stored in stores:

        @pl.when(stored)
        def _():
            pltpu.make_async_copy(staged.at[i, v], main.at[0], out_sems.at[i, v]).wait()

    for store in table_stores:
        store.wait()


def pack(views, owners, blocks_of, here, peers, groups):
    blocks, nviews, depth, lat = views.shape
    assert peers * CAP < lat
    return pl.pallas_call(
        pack_kernel,
        out_shape=(jax.ShapeDtypeStruct((peers * MAIN, depth, lat), views.dtype),)
        + (jax.ShapeDtypeStruct((1, depth + TILE, lat), views.dtype),) * groups,
        in_specs=[SMEM, SMEM, SMEM, ANY],
        out_specs=(ANY,) * (1 + groups),
        scratch_shapes=[
            pltpu.SMEM((peers * CAP + 1,), jnp.int32),
            pltpu.SMEM((peers,), jnp.int32),
            pltpu.SMEM((groups,), jnp.int32),
            pltpu.VMEM(views.shape, views.dtype),
            pltpu.VMEM((TILE, lat), views.dtype),
            pltpu.SemaphoreType.DMA((blocks, nviews)),
            pltpu.SemaphoreType.DMA((blocks, nviews)),
            pltpu.SemaphoreType.DMA((groups,)),
        ],
        name="pack",
    )(owners, blocks_of, here, views)


def all_thirds_kernel(owners, views, out, seen, staged, sems):
    blocks, nviews = views.shape[0], views.shape[1]

    @pl.loop(0, out.shape[0])
    def _(peer):
        seen[peer] = 0

    for i in range(blocks):
        for v in range(nviews):
            owner = owners[i, v]
            order = seen[owner]
            seen[owner] = order + 1

            @pl.when(order >= MAIN)
            def _():
                load = pltpu.make_async_copy(views.at[i, v], staged, sems.at[0])
                load.start()
                load.wait()
                store = pltpu.make_async_copy(staged, out.at[owner], sems.at[1])
                store.start()
                store.wait()


def pack_all_thirds(views, owners, peers):
    depth, lat = views.shape[2:]
    return pl.pallas_call(
        all_thirds_kernel,
        out_shape=jax.ShapeDtypeStruct((peers, depth, lat), views.dtype),
        in_specs=[SMEM, ANY],
        out_specs=ANY,
        scratch_shapes=[
            pltpu.SMEM((peers,), jnp.int32),
            pltpu.VMEM((depth, lat), views.dtype),
            pltpu.SemaphoreType.DMA((2,)),
        ],
        name="all_thirds",
    )(owners, views)


def group_count(peers):
    members = 1
    while peers % (2 * members) == 0 and members * members < peers:
        members *= 2
    return peers // members


def along_groups(rows):
    peers = lax.axis_size("join")
    members = peers // len(rows)
    line = [rows[0]]
    for k in range(1, len(rows)):
        line.append(
            lax.ppermute(rows[k], "join", [(i, (i + k * members) % peers) for i in range(peers)])
        )
    return line


def among_members(line):
    peers = lax.axis_size("join")
    members = peers // len(line)
    line = jnp.concatenate(line, axis=0)
    parts = [line]
    for m in range(1, members):
        parts.append(lax.ppermute(line, "join", [(i, i ^ m) for i in range(peers)]))
    return parts


def sources_of_parts(groups):
    peers = lax.axis_size("join")
    members = peers // groups
    here = lax.axis_index("join")
    at = jnp.arange(peers, dtype=jnp.int32)
    group = lax.rem(here // members + groups - lax.rem(at, groups), groups)
    return group * members + jnp.bitwise_xor(lax.rem(here, members), at // groups)


def ends_kernel(start, *refs):
    blocks, (out, staged, sems) = refs[:-3], refs[-3:]
    width = out.shape[1]
    copies, first = [], 0
    for k, block in enumerate(blocks):
        number = block.shape[0]
        held = staged.at[pl.ds(first, number)]
        rows = block.at[:, pl.ds(pl.multiple_of(start[0], TILE), width)]
        copies.append(
            (
                pltpu.make_async_copy(rows, held, sems.at[0, k]),
                pltpu.make_async_copy(held, out.at[pl.ds(first, number)], sems.at[1, k]),
            )
        )
        first += number
    for load, _ in copies:
        load.start()
    for load, store in copies:
        load.wait()
        store.start()
    for _, store in copies:
        store.wait()


def ends(blocks, start, width):
    if len(blocks) == 1:
        return lax.dynamic_slice_in_dim(blocks[0], start, width, axis=1)
    shape = (sum(block.shape[0] for block in blocks), width, blocks[0].shape[2])
    return pl.pallas_call(
        ends_kernel,
        out_shape=jax.ShapeDtypeStruct(shape, blocks[0].dtype),
        in_specs=[SMEM] + [ANY] * len(blocks),
        out_specs=ANY,
        scratch_shapes=[
            pltpu.VMEM(shape, blocks[0].dtype),
            pltpu.SemaphoreType.DMA((2, len(blocks))),
        ],
        name="ends",
    )(jnp.asarray(start, jnp.int32)[None], *blocks)


def halos(blocks, depth, width):
    count = lax.axis_size("view")
    if count == 1:
        return []
    if count == 2:
        sent = ends(blocks, jnp.where(lax.axis_index("view") == 0, depth - width, 0), width)
        return [lax.ppermute(sent, "view", [(0, 1), (1, 0)])]
    forward = [(i, i + 1) for i in range(count - 1)]
    backward = [(target, source) for source, target in forward]
    low = lax.ppermute(ends(blocks, depth - width, width), "view", forward)
    high = lax.ppermute(ends(blocks, 0, width), "view", backward)
    return [low, high]


def framed(block, sides, dim):
    if not sides:
        return block
    if len(sides) == 2:
        return jnp.concatenate([sides[0], block, sides[1]], axis=dim)
    (side,) = sides
    return jnp.where(
        lax.axis_index("view") == 0,
        jnp.concatenate([block, side], axis=dim),
        jnp.concatenate([side, block], axis=dim),
    )


def low_rows():
    count = lax.axis_size("view")
    if count == 2:
        return jnp.where(lax.axis_index("view") == 0, 0, H).astype(jnp.int32)
    return jnp.int32(0 if count == 1 else H)


def halo_rows(sweep):
    return VIEW_HALO - 2 * H * sweep


def piece_starts(depth, sweep):
    count = lax.axis_size("view")
    width = halo_rows(sweep)
    if count == 1:
        return [jnp.int32(0)]
    if count == 2:
        first = lax.axis_index("view") == 0
        return [jnp.where(first, 0, width), jnp.where(first, depth, 0)]
    return [jnp.int32(width), jnp.int32(0), jnp.int32(width + depth)]


def bands_kernel(shapes, shifts, taps_rows, *refs):
    width = taps_rows.shape[-1]
    nviews = taps_rows.shape[1]

    def band(which, v, shift, rows):
        spread = jnp.broadcast_to(taps_rows[which, v : v + 1, :], (rows, width))
        return pltpu.roll(pltpu.roll(spread, 0, 1, stride=1, stride_axis=0), shift, 1)

    at = 0
    for sweep, pieces in enumerate(shapes):
        forward, mirror = refs[2 * sweep], refs[2 * sweep + 1]
        columns, outs = forward.shape[2], mirror.shape[1]
        lane = lax.broadcasted_iota(jnp.int32, (outs, width), 1)
        for v in range(nviews):
            total = jnp.zeros((outs, width), jnp.float32)
            first = 0
            for piece, rows in enumerate(pieces):
                part = band(0, v, shifts[at + 2 * piece], rows)
                forward[v, first : first + rows] = part[:, :columns].astype(forward.dtype)
                inside = jnp.logical_and(lane >= first, lane < first + rows)
                total = jnp.where(inside, band(1, v, shifts[at + 2 * piece + 1], outs), total)
                first += rows
            mirror[v] = total[:, :first].astype(mirror.dtype)
        at += 2 * len(pieces)


def bands(kernel, depth, sides):
    nviews, taps = kernel.shape
    low = low_rows()
    frame = depth + sides * EST_HALO
    width = -(-(frame + 4 * H) // 128) * 128
    shapes, shifts, outs = [], [], []
    for sweep in range(ITERS):
        pieces = (depth,) + (halo_rows(sweep),) * sides
        first = 0
        for rows, start in zip(pieces, piece_starts(depth, sweep)):
            shifts.append(lax.rem(start + low - H + width, width))
            shifts.append(lax.rem(first - start + low - H + width, width))
            first += rows
        shapes.append(pieces)
        rows_in = frame - 2 * sides * H * sweep
        outs.append(jax.ShapeDtypeStruct((nviews, first, rows_in), jnp.bfloat16))
        outs.append(jax.ShapeDtypeStruct((nviews, rows_in - 2 * sides * H, first), jnp.bfloat16))
    rows = jnp.stack([kernel, kernel[:, ::-1]]).astype(jnp.float32)
    rows = jnp.pad(rows, ((0, 0), (0, 0), (0, width - taps)))
    return pl.pallas_call(
        functools.partial(bands_kernel, shapes),
        out_shape=outs,
        in_specs=[SMEM, VMEM],
        out_specs=[VMEM] * len(outs),
        cost_estimate=pl.CostEstimate(flops=10**11, bytes_accessed=0, transcendentals=0),
        name="bands",
    )(jnp.stack(shifts).astype(jnp.int32), rows)


def list_starts(peers):
    main, third = peers * MAIN + GROUP, peers + GROUP
    return 0, main, 2 * main, 2 * main + third, 2 * main + 2 * third, 2 * main + 3 * third


def plan_kernel(nviews, blocks, place, source, *refs):
    parts, (lists, any_crowded, tables, rows, scalars, sems) = refs[:-6], refs[-6:]
    per_part, depth, lat = parts[0].shape
    depth -= TILE
    peers = source.shape[0]
    blank = blocks * nviews
    main_slot, main_code, third_slot, third_source, third_code, numbers = list_starts(peers)
    loads = [
        pltpu.make_async_copy(
            part.at[:, pl.ds(depth, TILE)], tables.at[pl.ds(j * per_part, per_part)], sems.at[j]
        )
        for j, part in enumerate(parts)
    ]
    for load in loads:
        load.start()
    lists[numbers + 2] = place[1]
    for b in range(blocks):
        lists[numbers + 3 + b] = 0
    for load in loads:
        load.wait()
    at = lax.broadcasted_iota(jnp.int32, (peers, lat), 0)
    together = jnp.zeros((peers, lat), jnp.float32)
    for t in range(peers):
        row = jnp.broadcast_to(tables[t, :1].astype(jnp.float32), (peers, lat))
        together = jnp.where(at == t, row, together)
    rows[...] = together.astype(jnp.int32)
    copy = pltpu.make_async_copy(rows, scalars, sems.at[len(parts)])
    copy.start()
    copy.wait()

    def enlist(t, carry):
        in_main, in_third, crowded = carry
        for order in range(CAP):
            code = scalars[t, place[0] * CAP + order]
            valid = code >= 0

            @pl.when(valid)
            def _():
                at = numbers + 3 + code // nviews
                lists[at] = lists[at] + 1
                if order < MAIN:
                    lists[main_slot + in_main] = source[t] * MAIN + order
                    lists[main_code + in_main] = code
                else:
                    lists[third_slot + in_third] = t
                    lists[third_source + in_third] = source[t]
                    lists[third_code + in_third] = code

            if order < MAIN:
                in_main = in_main + valid.astype(jnp.int32)
            else:
                in_third = in_third + valid.astype(jnp.int32)
        return in_main, in_third, jnp.maximum(crowded, scalars[t, peers * CAP])

    zero = jnp.int32(0)
    in_main, in_third, crowded = lax.fori_loop(0, peers, enlist, (zero, zero, zero))
    lists[numbers] = in_main
    lists[numbers + 1] = in_third
    any_crowded[0] = crowded
    for more in range(GROUP - 1):
        lists[main_slot + in_main + more] = lists[main_slot]
        lists[main_code + in_main + more] = blank
        lists[third_slot + in_third + more] = lists[third_slot]
        lists[third_source + in_third + more] = lists[third_source]
        lists[third_code + in_third + more] = blank


def plan(parts, source, here, blocks, nviews):
    peers = source.shape[0]
    lat = parts[0].shape[-1]
    length = list_starts(peers)[-1] + 3 + blocks
    return pl.pallas_call(
        functools.partial(plan_kernel, nviews, blocks),
        out_shape=(
            jax.ShapeDtypeStruct((length,), jnp.int32),
            jax.ShapeDtypeStruct((1,), jnp.int32),
        ),
        in_specs=[SMEM] * 2 + [ANY] * len(parts),
        out_specs=(SMEM,) * 2,
        scratch_shapes=[
            pltpu.VMEM((peers, TILE, lat), parts[0].dtype),
            pltpu.VMEM((peers, lat), jnp.int32),
            pltpu.SMEM((peers, lat), jnp.int32),
            pltpu.SemaphoreType.DMA((len(parts) + 1,)),
        ],
        name="plan",
    )(jnp.stack([here, low_rows()]), source, *parts)


def deconvolve_kernel(starts, nparts, sides, guard, listed, main, est, *refs):
    main_slot, main_code, third_slot, third_code, numbers = starts
    parts, third_halo, refs = refs[:nparts], refs[nparts : nparts + sides], refs[nparts + sides :]
    number = 2 * ITERS + sides
    sources, out, refs = refs[:number], refs[number], refs[number + 1 :]
    copied, refs = refs[:number], refs[number:]
    bands_of, main_halo = copied[: 2 * ITERS], copied[2 * ITERS :]
    lists, held, *refs = refs
    held_halo, refs = refs[:sides], refs[sides:]
    recip, following, total, result, own_sems, held_sems, out_sems, lists_sem = refs
    blocks, depth, lat = out.shape
    nviews = bands_of[0].shape[0]
    own = [
        pltpu.make_async_copy(source, to, own_sems.at[k])
        for k, (source, to) in enumerate(zip(sources, copied))
    ]
    own[0].start()
    listing = pltpu.make_async_copy(listed, lists, lists_sem)
    listing.start()
    for copy in own[1:]:
        copy.start()
    number, part_rows = parts[0].shape[0], parts[0].shape[1]
    third_copies = [
        pltpu.make_async_copy(
            part, held.at[pl.ds(j * number, number), pl.ds(0, part_rows)], held_sems.at[j]
        )
        for j, part in enumerate(parts)
    ] + [
        pltpu.make_async_copy(ref, to, held_sems.at[nparts + side])
        for side, (ref, to) in enumerate(zip(third_halo, held_halo))
    ]
    recip[blocks * nviews] = jnp.zeros(recip.shape[1:], recip.dtype)
    stores = []
    for sweep in range(ITERS):
        current = est if sweep == 0 else following
        forward, mirror = bands_of[2 * sweep], bands_of[2 * sweep + 1]
        next_rows, view_rows = mirror.shape[1], mirror.shape[2]
        side_rows = halo_rows(sweep)
        own[2 * sweep].wait()
        seen_blocks = range(blocks)
        if sweep > 0 and blocks > 2:
            unseen = jnp.int32(blocks - 2)
            for b in reversed(range(1, blocks - 2)):
                unseen = jnp.where(counts[b] == 0, b, unseen)
            seen_blocks = [b + (b >= unseen).astype(jnp.int32) for b in range(blocks - 1)]
        for b in seen_blocks:
            rounded = current[b, : forward.shape[2]].astype(jnp.bfloat16)
            for v in range(nviews):
                blurred = jnp.dot(forward[v], rounded, preferred_element_type=jnp.float32)
                inverse = 1.0 / blurred
                if guard:
                    inverse = jnp.where(blurred > 0, inverse, 0.0)
                recip[b * nviews + v, :view_rows] = inverse

        if sweep == 0:
            listing.wait()
            mains, thirds = lists[numbers], lists[numbers + 1]
            low = pl.multiple_of(lists[numbers + 2], H)
            counts = [lists[numbers + 3 + b] for b in range(blocks)]

            @pl.when(thirds > 0)
            def _():
                for copy in third_copies:
                    copy.start()

        next_at = pl.multiple_of(2 * low, 2 * H)
        halo_at = [pl.multiple_of(2 * sweep * low, 2 * H), 0]
        total[:, :next_rows] = jnp.zeros((blocks + 1, next_rows, lat), jnp.float32)

        def main_rows(p):
            slot = lists[main_slot + p]
            rows = [main[slot]]
            for side, ref in enumerate(main_halo):
                rows.append(ref[slot, pl.ds(halo_at[side], side_rows)])
            return rows

        def third_rows(p):
            slot = lists[third_slot + p]
            rows = [held[slot, :depth]]
            for side, ref in enumerate(held_halo):
                rows.append(ref[slot, pl.ds(halo_at[side], side_rows)])
            return rows

        def add(number, rows_of, code_at):
            wide = (number + (SMALL - 1)) // GROUP
            pl.loop(0, wide)(lambda group: add_group(group * GROUP, GROUP, rows_of, code_at))

            @pl.when(number > wide * GROUP)
            def _():
                add_group(wide * GROUP, SMALL, rows_of, code_at)

        def add_group(first_entry, size, rows_of, code_at):
            gained = []
            for member in range(size):
                p = first_entry + member
                code = lists[code_at + p]
                b = code // nviews
                pieces, first = [], 0
                for rows in rows_of(p):
                    last = first + rows.shape[0]
                    quotient = rows.astype(jnp.float32) * recip[code, first:last]
                    pieces.append(quotient.astype(jnp.bfloat16))
                    first = last
                part = jnp.dot(
                    mirror[code - b * nviews],
                    jnp.concatenate(pieces, axis=0),
                    preferred_element_type=jnp.float32,
                )
                gained.append((b, part))
            for b, part in gained:
                total[b, :next_rows] += part

        own[2 * sweep + 1].wait()
        if sweep == 0:
            for copy in own[2 * ITERS :]:
                copy.wait()
        add(mains, main_rows, main_code)
        if sweep == 0:

            @pl.when(thirds > 0)
            def _():
                for copy in third_copies:
                    copy.wait()

        add(thirds, third_rows, third_code)
        for b in range(blocks):
            average = total[b, :next_rows] / jnp.maximum(counts[b], 1).astype(jnp.float32)
            factor = jnp.where(counts[b] > 0, average, 1.0)
            updated = current[b, pl.ds(next_at, next_rows)] * factor
            if sweep < ITERS - 1:
                following[b, :next_rows] = updated
            else:
                result[b] = updated
                store = pltpu.make_async_copy(result.at[b], out.at[b], out_sems.at[b])
                store.start()
                stores.append(store)
    for store in stores:
        store.wait()


def deconvolve(lists, starts, main, parts, main_halo, third_halo, est, matrices, depth, guard):
    blocks, frame, lat = est.shape
    nviews, view_rows = matrices[0].shape[:2]
    sides = len(main_halo)
    following = (frame - 2 * sides * H, lat)
    third_halo_shape = (len(parts) * parts[0].shape[0], VIEW_HALO, lat)
    copied = [*matrices, *main_halo]
    in_place = [*parts, *third_halo, *copied]
    return pl.pallas_call(
        functools.partial(deconvolve_kernel, starts, len(parts), sides, guard),
        out_shape=pltpu.HBM((blocks, depth, lat), jnp.float32),
        in_specs=[ANY] + [VMEM] * 2 + [ANY] * len(in_place),
        out_specs=HBM,
        scratch_shapes=[pltpu.VMEM(array.shape, array.dtype) for array in copied]
        + [
            pltpu.SMEM(lists.shape, lists.dtype),
            pltpu.VMEM((third_halo_shape[0], depth + TILE, lat), main.dtype),
        ]
        + [pltpu.VMEM(third_halo_shape, main.dtype)] * sides
        + [
            pltpu.VMEM((blocks * nviews + 1, view_rows, lat), jnp.float32),
            pltpu.VMEM((blocks, *following), jnp.float32),
            pltpu.VMEM((blocks + 1, *following), jnp.float32),
            pltpu.VMEM((blocks, depth, lat), jnp.float32),
            pltpu.SemaphoreType.DMA((len(copied),)),
            pltpu.SemaphoreType.DMA((len(parts) + sides,)),
            pltpu.SemaphoreType.DMA((blocks,)),
            pltpu.SemaphoreType.DMA,
        ],
        compiler_params=pltpu.CompilerParams(vmem_limit_bytes=24 * 1024 * 1024),
        name="deconvolve",
    )(lists, main, est, *in_place)


def local(estimate, views, owners, local_blocks, psf):
    blocks, depth, lat = estimate.shape
    nviews = views.shape[1]
    peers = lax.axis_size("join")
    groups = group_count(peers)
    here = lax.axis_index("join").astype(jnp.int32)
    normed = psf / jnp.sum(psf, axis=1, keepdims=True)
    kernel = normed.astype(jnp.bfloat16)

    packed, *rows = pack(
        views, owners, local_blocks, (here // (peers // groups))[None], peers, groups
    )
    line = along_groups(rows)
    arrived = lax.all_to_all(
        packed.reshape(peers, MAIN, depth, lat), "join", split_axis=0, concat_axis=0, tiled=True
    ).reshape(peers * MAIN, depth, lat)

    parts = among_members(line)
    source = sources_of_parts(groups)
    kernel, estimate, line = lax.optimization_barrier((kernel, estimate, line))
    est_halos = halos([estimate], depth, EST_HALO)
    est = framed(estimate, est_halos, 1)
    matrices = bands(kernel, depth, len(est_halos))
    parts, source, est, matrices = lax.optimization_barrier((parts, source, est, matrices))
    third_halo = halos(parts, depth, VIEW_HALO)
    planned = plan(parts, source, here, blocks, nviews)
    arrived, parts, third_halo, planned, est, matrices = lax.optimization_barrier(
        (arrived, parts, third_halo, planned, est, matrices)
    )
    lists, any_crowded = planned
    main_slot, main_code, third_slot, third_source, third_code, numbers = list_starts(peers)

    main_halo = halos([arrived], depth, VIEW_HALO)
    guard = lax.axis_size("view") > 2

    def finish(third_at, thirds, third_halo):
        return deconvolve(
            lists,
            (main_slot, main_code, third_at, third_code, numbers),
            arrived,
            thirds,
            main_halo,
            third_halo,
            est,
            matrices,
            depth,
            guard,
        )

    def fallback():
        sent = pack_all_thirds(views, owners, peers)
        thirds = lax.all_to_all(sent, "join", split_axis=0, concat_axis=0, tiled=True)
        return finish(third_source, [thirds], halos([thirds], depth, VIEW_HALO))

    return lax.cond(
        any_crowded[0] > 0, fallback, lambda: finish(third_slot, parts, third_halo)
    )


def solution(mesh):
    in_specs = (
        P("join", "view", None),
        P("join", None, "view", None),
        P("join", None),
        P("join", None),
        P(),
    )
    out_specs = P("join", "view", None)
    return jax.shard_map(local, mesh=mesh, in_specs=in_specs, out_specs=out_specs, check_vma=False)
```
